256 devices in a mesh: gx: 4 (over x), gy: 8 (over z), gz: 8 (over y, core).
Axes of the slice: x: 4, y: 4, z: 8, core: 2. Of those that a mesh axis runs over, the one named last changes fastest.
Arguments:
- solution: float32 [4, 8, 32, 64, 1024], P(None, None, 'gx', 'gy', 'gz'), may hold values from -6 to 6
- residual: float32 [4, 8, 32, 64, 1024], P(None, None, 'gx', 'gy', 'gz'), may hold values from -21 to 21
- permeability: float32 [4, 32, 64, 1024], P(None, 'gx', 'gy', 'gz'), may hold values from 0.1 to 1
- storage: float32 [4, 32, 64, 1024], P(None, 'gx', 'gy', 'gz'), may hold values from 0.5 to 2
- tissue_mask: int32 [32, 64, 1024], P('gx', 'gy', 'gz'), may hold values 0 or 1
- tissue_label: int32 [32, 64, 1024], P('gx', 'gy', 'gz'), may hold values from 0 to 2
- exchange_table: float32 [3, 6], replicated, may hold values from 0.2 to 1
Outputs:
- new_solution: float32 [4, 8, 32, 64, 1024], P(None, None, 'gx', 'gy', 'gz')
- new_residual: float32 [4, 8, 32, 64, 1024], P(None, None, 'gx', 'gy', 'gz')
- basis: float32 [4, 32, 32, 64, 1024], P(None, None, 'gx', 'gy', 'gz')
The draws below stay inside these ranges and needn't reach their ends.
All inputs are finite; a program needn't handle non-finite values. No bound on the sum of `tissue_mask` on one device may be relied on, other than what follows from the above.
Results may differ from the reference program's by a relative error of at most 0.027.
Values sent between devices are 32-bit elements; how exact they have to be, the bound alone decides.
No kernel may reach another device: no remote copies, remote signals or barrier semaphores. Data moves between devices by JAX's collectives and lax.ppermute only.
A program may use at most 128 MiB of HBM per device.

```python
import math
import jax
import jax.numpy as jnp
import numpy as np
from jax import lax

COMP = 4
RHS = 8
S = 4
NX = 32
NY = 64
NZ = 1024


def draw_residual(key, part):
    positions = jnp.arange(NX, dtype=jnp.float32) / max(NX - 1, 1)
    values = jnp.clip(jax.random.normal(key, (COMP, RHS, NX, NY, NZ), jnp.float32), -6.0, 6.0)
    ramp = 1.0 + 2.0 * positions
    return (values * ramp[:, None, None]).astype(jnp.float32)


def plant(entries, key, least, high):
    shape = entries.shape
    place = [jax.random.randint(jax.random.fold_in(key, axis), (), 0, shape[axis]) for axis in range(len(shape))]
    entries = entries.at[tuple(place)].set(least)
    longest = shape.index(max(shape))
    place[longest] = (place[longest] + 1) % shape[longest]
    return entries.at[tuple(place)].set(high)


def block_levels(stream_key, shape, split, smallest, high):
    loudness, own = 1.0, jax.random.fold_in(stream_key, 6)
    for dim, parts in split:
        steps = jnp.exp(jax.random.uniform(jax.random.fold_in(own, dim), (parts,), jnp.float32, smallest / len(split), high / len(split)))
        loudness = loudness * jnp.repeat(steps, shape[dim] // parts).reshape([-1 if axis == dim else 1 for axis in range(len(shape))])
    return loudness


def bell_draw(own_key, dims, deviation, limit, cuts=(), kind=jnp.bfloat16):
    level = block_levels(own_key, dims, cuts, -0.22, 0.18) if cuts else 1.0
    values = jax.random.normal(own_key, dims, jnp.float32) * deviation * level
    return jnp.minimum(jnp.maximum(values, -limit), limit).astype(kind)


def setup_inputs(seed: int = 0) -> dict:
    keys = jax.random.split(jax.random.key(seed), 8)
    solution = bell_draw(keys[0], (COMP, RHS, NX, NY, NZ), 1.0, 6.0, ((2, 4), (3, 8), (4, 8)), jnp.float32)
    residual = draw_residual(jax.random.fold_in(keys[7], 71), 0)
    permeability = jnp.clip(jnp.exp(math.log(1.0) - 2.3025851 * jax.random.uniform(keys[2], (COMP, NX, NY, NZ), jnp.float32) ** block_levels(keys[2], (COMP, NX, NY, NZ), ((1, 4), (2, 8), (3, 8)), -0.2, 0.2)), 0.1, 1.0)
    storage = jnp.clip(jnp.exp(math.log(2.0) - 1.3862944 * jax.random.uniform(keys[3], (COMP, NX, NY, NZ), jnp.float32) ** block_levels(keys[3], (COMP, NX, NY, NZ), ((1, 4), (2, 8), (3, 8)), -0.2, 0.2)), 0.5, 2.0)
    tissue_mask = plant((jax.random.randint(keys[4], (NX, NY, NZ), 0, 8) < 7).astype(jnp.int32), jax.random.fold_in(keys[4], 1), 0, 1)
    tissue_label = plant(jax.random.randint(keys[5], (NX, NY, NZ), 0, 3), jax.random.fold_in(keys[5], 1), 0, 2).astype(jnp.int32)
    exchange_table = jnp.clip(jnp.exp(jax.random.uniform(keys[6], (3, 6), jnp.float32, math.log(0.2), math.log(1.0))), 0.2, 1.0)
    return dict(solution=solution, residual=residual, permeability=permeability, storage=storage, tissue_mask=tissue_mask, tissue_label=tissue_label, exchange_table=exchange_table)


PAIRS = ((0, 1), (0, 2), (0, 3), (1, 2), (1, 3), (2, 3))
SHIFTS = (2.0, 14.0, 6.0, 10.0)
NEWTON_SCALE = 8.0
HIGHEST_PRECISION = lax.Precision.HIGHEST

def shifted(array, direction, offset):
    leading = array.ndim - 3
    index = [slice(None)] * leading
    for dimension in range(3):
        length = array.shape[leading + dimension]
        if dimension == direction:
            index.append(slice(offset, length - 2 + offset))
        else:
            index.append(slice(1, length - 1))
    return array[tuple(index)]

def interior(array):
    return shifted(array, 0, 1)

def padded(array):
    return jnp.pad(array, [(0, 0)] * (array.ndim - 3) + [(1, 1)] * 3)

def stencil(field, perm_pad, mask_pad, store_pad, rate_pad):
    centre = interior(field)
    perm_mid = interior(perm_pad)
    mask_mid = interior(mask_pad)
    result = interior(store_pad)[:, None] * centre
    for direction in range(3):
        for offset in (0, 2):
            faces = 0.5 * (perm_mid + shifted(perm_pad, direction, offset)) * (mask_mid * shifted(mask_pad, direction, offset))
            result = result + faces[:, None] * (centre - shifted(field, direction, offset))
    rate_mid = interior(rate_pad)
    pieces = [result[number] for number in range(4)]
    for number, pair in enumerate(PAIRS):
        flow = rate_mid[number] * (centre[pair[0]] - centre[pair[1]])
        pieces[pair[0]] = pieces[pair[0]] + flow
        pieces[pair[1]] = pieces[pair[1]] - flow
    return jnp.stack(pieces)

def apply_padded(field_pad, coeff_pad):
    return stencil(field_pad, coeff_pad[0:4], coeff_pad[14], coeff_pad[4:8], coeff_pad[8:14])

def build_coefficients(permeability, storage, tissue_mask, tissue_label, exchange_table):
    mask_float = tissue_mask.astype(jnp.float32)
    rates = jnp.zeros((6,) + tissue_mask.shape, jnp.float32)
    for level in range(3):
        weight = (tissue_label == level).astype(jnp.float32)
        rates = rates + exchange_table[level][:, None, None, None] * weight[None]
    rates = rates * mask_float[None]
    return jnp.concatenate([permeability, storage, rates, mask_float[None]], 0)

def newton_table(steps, rhs_count):
    table = np.zeros(((steps + 1) * rhs_count, steps * rhs_count), np.float32)
    for index in range(steps):
        table[index * rhs_count:(index + 1) * rhs_count, index * rhs_count:(index + 1) * rhs_count] = SHIFTS[index] * np.eye(rhs_count)
        table[(index + 1) * rhs_count:(index + 2) * rhs_count, index * rhs_count:(index + 1) * rhs_count] = NEWTON_SCALE * np.eye(rhs_count)
    return jnp.asarray(table)

def local_gram(blocks):
    stacked = jnp.stack(blocks)
    flat = stacked.reshape(stacked.shape[0], stacked.shape[1], stacked.shape[2], -1)
    gram = jnp.einsum('kcjm,lcim->kjli', flat, flat, precision=HIGHEST_PRECISION)
    total = stacked.shape[0] * stacked.shape[2]
    return gram.reshape(total, total)

def lower_factor(matrix):
    extent = matrix.shape[0]
    positions = jnp.arange(extent)
    columns = []
    for col_index in range(extent):
        column = matrix[:, col_index]
        for inner in range(col_index):
            column = column - columns[inner] * columns[inner][col_index]
        pivot_value = jnp.sqrt(column[col_index])
        column = jnp.where(positions >= col_index, column / pivot_value, jnp.zeros_like(column))
        columns.append(column)
    return jnp.stack(columns, 1)

def lower_inverse(lower):
    extent = lower.shape[0]
    identity = jnp.eye(extent, dtype=lower.dtype)
    solved_rows = []
    for row_index in range(extent):
        current_row = identity[row_index]
        for inner in range(row_index):
            current_row = current_row - lower[row_index, inner] * solved_rows[inner]
        solved_rows.append(current_row / lower[row_index, row_index])
    return jnp.stack(solved_rows, 0)

def matmul(left, right):
    return jnp.dot(left, right, precision=HIGHEST_PRECISION)

def project(gram, steps, rhs_count):
    width = steps * rhs_count
    table = newton_table(steps, rhs_count)
    leading = gram[:width, :width]
    leading = 0.5 * (leading + leading.T)
    lower_inv = lower_inverse(lower_factor(leading))
    moment = matmul(gram[:width, :], table)
    moment = 0.5 * (moment + moment.T)
    projected = matmul(matmul(lower_inv, moment), lower_inv.T)
    projected = 0.5 * (projected + projected.T)
    right_part = matmul(lower_inv, gram[:width, :rhs_count])
    proj_inv = lower_inverse(lower_factor(projected))
    solved = matmul(proj_inv.T, matmul(proj_inv, right_part))
    inverse = lower_inv.T
    coeff = matmul(inverse, solved)
    extended = matmul(table, coeff)
    return (inverse, coeff, extended)

def finish(solution, residual, blocks, inverse, coeff, extended, steps, rhs_count):
    stacked = jnp.stack(blocks)
    flat = stacked.reshape(stacked.shape[0], stacked.shape[1], stacked.shape[2], -1)
    basis = jnp.einsum('kcjm,kjq->cqm', flat[:steps], inverse.reshape(steps, rhs_count, -1), precision=HIGHEST_PRECISION)
    basis = basis.reshape((stacked.shape[1], steps * rhs_count) + stacked.shape[3:])
    update = jnp.einsum('kcjm,kji->cim', flat[:steps], coeff.reshape(steps, rhs_count, rhs_count), precision=HIGHEST_PRECISION)
    image = jnp.einsum('kcjm,kji->cim', flat, extended.reshape(steps + 1, rhs_count, rhs_count), precision=HIGHEST_PRECISION)
    return (solution + update.reshape(solution.shape), residual - image.reshape(residual.shape), basis)

def reference(solution, residual, permeability, storage, tissue_mask, tissue_label, exchange_table):
    coefficients = padded(build_coefficients(permeability, storage, tissue_mask, tissue_label, exchange_table))
    current = residual
    blocks = [residual]
    for index in range(S):
        applied = apply_padded(padded(current), coefficients)
        current = (applied - SHIFTS[index] * current) / NEWTON_SCALE
        blocks.append(current)
    gram = local_gram(blocks)
    inverse, coeff, extended = project(gram, S, RHS)
    return finish(solution, residual, blocks, inverse, coeff, extended, S, RHS)
```

```python
import jax
import jax.numpy as jnp
from jax import lax
from jax.experimental import pallas as pl
from jax.experimental.pallas import tpu as pltpu
from jax.sharding import PartitionSpec as P

COMP = 4
RHS = 8
S = 4
PAIRS = ((0, 1), (0, 2), (0, 3), (1, 2), (1, 3), (2, 3))
SHIFTS = (2.0, 14.0, 6.0, 10.0)
SCALE = 8.0
F32 = jnp.float32
BF16 = jnp.bfloat16

NX, NY, NZ = 8, 8, 128
FACE = COMP * 8
BLOCKS = tuple((a, b) for b in range(5) for a in range(min(b, 3) + 1))
VMEM = pl.BlockSpec(memory_space=pltpu.VMEM)
SMEM = pl.BlockSpec(memory_space=pltpu.SMEM)


def pair_index(a, b):
    return PAIRS.index((min(a, b), max(a, b)))


def lane_ids(shape):
    return lax.broadcasted_iota(jnp.int32, shape, len(shape) - 1)


def put_ends(acc, tile, lane, slot):
    return jnp.where((lane >> 1) == slot, pltpu.roll(tile, 2 * slot + 1, 1), acc)


def fetch(pairs, sems):
    copies = [pltpu.make_async_copy(src, dst, sems.at[i]) for i, (src, dst) in enumerate(pairs)]
    for copy in copies:
        copy.start()
    return copies


def pack_kernel(edge, res_hbm, perm_hbm, mask_hbm, v0, xlo, xhi, ylo, yhi, ends, pm, res, mask, sems):
    lane = lane_ids((8, NZ))
    copies = fetch(
        [(perm_hbm, pm.at[pl.ds(0, COMP)]), (mask_hbm, mask), (res_hbm, res)], sems
    )
    for f in range(COMP + 5):
        ends[f] = jnp.zeros((8, NZ), F32)
    copies[0].wait()
    copies[1].wait()

    def loop_coef(x, _):
        pm[COMP, x] = mask[x].astype(F32)
        for f in range(5):
            tile = pm[f, x]
            ylo[FACE + f, pl.ds(x, 1), :] = tile[0:1]
            yhi[FACE + f, pl.ds(x, 1), :] = tile[7:8]
            acc = put_ends(jnp.zeros((8, NZ), F32), tile, lane, 0)
            ends[COMP + f] = jnp.where((lane >> 1) == x, pltpu.roll(acc, 2 * x, 1), ends[COMP + f])
        return 0

    lax.fori_loop(0, NX, loop_coef, 0)
    for f in range(5):
        xlo[FACE + f] = pm[f, 0]
        xhi[FACE + f] = pm[f, NX - 1]
    copies[2].wait()

    def loop(x, _):
        for c in range(COMP):
            acc = jnp.zeros((8, NZ), F32)
            for y in range(NY):
                tile = res[pl.ds(c * 512 + x * 8 + y, 8, stride=64), :]
                v0[c, x, y] = tile
                acc = put_ends(acc, tile, lane, y)
                if y == 0:
                    ylo[c * 8 + x] = tile
                if y == NY - 1:
                    yhi[c * 8 + x] = tile
            ends[c] = jnp.where((lane >> 4) == x, pltpu.roll(acc, 16 * x, 1), ends[c])
        return 0

    lax.fori_loop(0, NX, loop, 0)
    for c in range(COMP):
        for y in range(NY):
            xlo[c * 8 + y] = v0[c, 0, y]
            xhi[c * 8 + y] = v0[c, NX - 1, y]


def prepare_kernel(table, pm, sol_hbm, store_hbm, label_hbm, sol, rate, base, label, sems):
    copies = fetch([(store_hbm, base), (label_hbm, label), (sol_hbm, sol)], sems)
    copies[0].wait()
    copies[1].wait()

    def loop(x, _):
        m = pm[COMP, x] * (1.0 / SCALE)
        kind = label[x]
        rates = []
        for q in range(6):
            value = jnp.where(kind == 0, table[0, q], jnp.where(kind == 1, table[1, q], table[2, q]))
            rates.append(m * value)
            rate[q, x] = rates[q]
        for c in range(COMP):
            total = base[c, x] * (1.0 / SCALE)
            for b in range(COMP):
                if b != c:
                    total = total + rates[pair_index(c, b)]
            base[c, x] = total
        return 0

    lax.fori_loop(0, NX, loop, 0)
    copies[2].wait()


def coefficients(edge, inner, base, halo, tx, ty, tz, diag, pm, ghost):
    xl, xh, yl, yh, zl, zh = halo
    lane = lane_ids((8, NZ))
    sub = lax.broadcasted_iota(jnp.int32, (8, NZ), 0)
    keep = [edge[i].astype(F32) for i in range(6)]
    for f in range(5):
        last = f == 4
        pm[f, 0] = xl[FACE + f] * keep[0] if last else xl[FACE + f]
        pm[f, NX + 1] = xh[FACE + f] * keep[1] if last else xh[FACE + f]
        for x in range(NX):
            pm[f, x + 1] = inner[f, x]
        below, above = zl[COMP + f], zh[COMP + f]
        if last:
            below, above = below * keep[4], above * keep[5]
        ghost[f] = jnp.where((lane & 1) == 0, below, above)

    def loop(x, _):
        m = pm[4, x + 1]
        def near(f, own):
            g = pltpu.roll(ghost[f], (127 - 2 * x) & 127, 1)
            row_lo = yl[FACE + f, pl.ds(x, 1), :]
            row_hi = yh[FACE + f, pl.ds(x, 1), :]
            if f == 4:
                row_lo, row_hi = row_lo * keep[2], row_hi * keep[3]
            y_lo = jnp.where(sub == 0, row_lo, pltpu.roll(own, 1, 0))
            y_hi = jnp.where(sub == 7, row_hi, pltpu.roll(own, 7, 0))
            z_lo = pltpu.roll(jnp.where(lane == 127, g, own), 1, 1)
            z_hi = pltpu.roll(jnp.where(lane == 0, g, own), 127, 1)
            return y_lo, y_hi, z_lo, z_hi

        masks = [m * n for n in near(4, m)]
        for c in range(COMP):
            own = pm[c, x + 1]
            values = [
                (-0.5 / SCALE) * (own + n) * mm for n, mm in zip(near(c, own), masks)
            ]
            x_lo = (-0.5 / SCALE) * (own + pm[c, x]) * (m * pm[4, x])
            x_hi = (-0.5 / SCALE) * (own + pm[c, x + 2]) * (m * pm[4, x + 2])
            tx[c, x] = x_lo
            tx[c, x + 1] = x_hi
            ty[c, x], ty[COMP + c, x] = values[0], values[1]
            tz[c, x], tz[COMP + c, x] = values[2], values[3]
            diag[c, x] = base[c, x] - values[0] - values[1] - values[2] - values[3] - x_lo - x_hi
        return 0

    lax.fori_loop(0, NX, loop, 0)


def apply_step(shift, cur, halo, tx, ty, tz, diag, rate, vp, ghost, out, sends):
    xl, xh, yl, yh, zl, zh = halo
    lane = lane_ids((8, NZ))
    first, last = lane == 0, lane == 127
    for c in range(COMP):
        for y in range(NY):
            vp[c, 0, y] = xl[c * 8 + y]
            vp[c, NX + 1, y] = xh[c * 8 + y]
        ghost[c] = jnp.where((lane & 1) == 0, zl[c], zh[c])

    def copy(x, _):
        for c in range(COMP):
            for y in range(NY):
                vp[c, x + 1, y] = cur[c, x, y]
        return 0

    lax.fori_loop(0, NX, copy, 0)
    if sends is not None:
        for c in range(COMP):
            sends[4][c] = jnp.zeros((8, NZ), F32)

    def loop(x, _):
        near_z = [pltpu.roll(ghost[c], (128 - 16 * x) & 127, 1) for c in range(COMP)]
        acc = [jnp.zeros((8, NZ), F32) for _ in range(COMP)]
        low = [yl[c * 8 + x] for c in range(COMP)]
        own = [vp[c, x + 1, 0] for c in range(COMP)]
        for y in range(NY):
            if y < NY - 1:
                high = [vp[c, x + 1, y + 1] for c in range(COMP)]
            else:
                high = [yh[c * 8 + x] for c in range(COMP)]
            rates = [rate[q, x, pl.ds(y, 1), :] for q in range(6)]
            for c in range(COMP):
                p = own[c]
                g = pltpu.roll(near_z[c], 127 - 2 * y, 1)
                z_lo = pltpu.roll(jnp.where(last, g, p), 1, 1)
                z_hi = pltpu.roll(jnp.where(first, g, p), 127, 1)
                row = pl.ds(y, 1)
                value = (diag[c, x, row, :] - shift / SCALE) * p
                side = tx[c, x, row, :] * vp[c, x, y] + tx[c, x + 1, row, :] * vp[c, x + 2, y]
                value = value + ty[c, x, row, :] * low[c]
                side = side + ty[COMP + c, x, row, :] * high[c]
                value = value + tz[c, x, row, :] * z_lo
                side = side + tz[COMP + c, x, row, :] * z_hi
                others = [b for b in range(COMP) if b != c]
                flow = rates[pair_index(c, others[0])] * own[others[0]]
                for b in others[1:]:
                    flow = flow + rates[pair_index(c, b)] * own[b]
                value = (value + side) - flow
                out[c, x, y] = value
                if sends is not None:
                    acc[c] = put_ends(acc[c], value, lane, y)
                    if y == 0:
                        sends[2][c * 8 + x] = value
                    if y == NY - 1:
                        sends[3][c * 8 + x] = value
            low, own = own, high
        if sends is not None:
            for c in range(COMP):
                sends[4][c] = jnp.where((lane >> 4) == x, pltpu.roll(acc[c], 16 * x, 1), sends[4][c])
        return 0

    lax.fori_loop(0, NX, loop, 0)
    if sends is not None:
        for c in range(COMP):
            for y in range(NY):
                sends[0][c * 8 + y] = out[c, 0, y]
                sends[1][c * 8 + y] = out[c, NX - 1, y]


def first_kernel(edge, piece, cur, inner, base, rate, *refs):
    halo, refs = refs[:6], refs[6:]
    out, sends, coef, scratch = refs[0], refs[1:6], refs[6:10], refs[10:]
    vp, ghost, pm, ghost_c = scratch
    coefficients(edge, inner, base, halo, *coef, pm, ghost_c)
    apply_step(SHIFTS[0], cur, halo, *coef, rate, vp, ghost, out, sends)


def step_kernel(index, piece, cur, *refs):
    halo, coef, refs = refs[:6], refs[6:11], refs[11:]
    out, refs = refs[0], refs[1:]
    sends = None
    if index < S - 1:
        sends, refs = refs[:5], refs[5:]
    apply_step(SHIFTS[index], cur, halo, *coef, *refs, out, sends)


def gram_kernel(index, cur, *refs):
    older, refs = refs[:index], refs[index:]
    before = None
    if index:
        before, refs = refs[0], refs[1:]
    split, out = refs
    lane = lane_ids((8, NZ))
    count = min(index, 3) + 1
    tall = 16 * count

    def loop(x, total):
        tiles = []
        for c in range(COMP):
            for y in range(NY):
                v = cur[c, x, y]
                high = v.astype(BF16).astype(F32)
                tile = jnp.concatenate([high, v - high], 0).astype(BF16)
                split[c, x, y] = tile
                tiles.append(tile)
        right = jnp.concatenate(tiles, 1)
        lefts = [
            jnp.concatenate([older[k][c, x, y] for c in range(COMP) for y in range(NY)], 1)
            for k in range(min(index, count))
        ]
        if count > index:
            lefts.append(right)
        left = jnp.concatenate(lefts, 0) if len(lefts) > 1 else lefts[0]
        return total + lax.dot_general(
            left, right, (((1,), (1,)), ((), ())), preferred_element_type=F32
        )

    total = lax.fori_loop(0, NX, loop, jnp.zeros((tall, 16), F32))
    wide = jnp.concatenate([total, jnp.zeros((tall, NZ - 16), F32)], 1)
    value = jnp.zeros((8, NZ), F32)
    for a in range(count):
        both = wide[16 * a : 16 * a + 8] + wide[16 * a + 8 : 16 * a + 16]
        both = both + pltpu.roll(both, NZ - 8, 1)
        slot = BLOCKS.index((a, index))
        value = jnp.where((lane >> 3) == slot, pltpu.roll(both, 8 * slot, 1), value)
    if index:
        value = value + before[...]
    if index < S:
        out[...] = value
    else:
        for copy in range(out.shape[0]):
            out[copy] = value


def relay_kernel(parts, out):
    total = parts[0]
    for i in range(1, parts.shape[0]):
        total = total + parts[i]
    for copy in range(out.shape[0]):
        out[copy] = total


def lane_group(tile, source, target):
    return pltpu.roll(tile, (8 * (target - source)) % NZ, 1)


def factor(packed, weight):
    lane8 = lane_ids((8, NZ)) >> 3
    turned = jnp.transpose(jnp.concatenate([packed, jnp.zeros((NZ - 8, NZ), F32)], 0))
    rows = []
    for a in range(S):
        line = jnp.zeros((8, NZ), F32)
        for b in range(S + 1):
            if a <= b:
                block = lane_group(packed, BLOCKS.index((a, b)), b)
            else:
                slot = BLOCKS.index((b, a))
                block = lane_group(turned[8 * slot : 8 * slot + 8], 0, b)
            if a == b:
                slot = BLOCKS.index((a, a))
                other = lane_group(turned[8 * slot : 8 * slot + 8], 0, b)
                block = 0.5 * (block + other)
            line = jnp.where(lane8 == b, block, line)
        rows.append(line)
    gram = jnp.concatenate(rows, 0)
    lane = lane_ids((32, NZ))
    row = lax.broadcasted_iota(jnp.int32, (32, NZ), 0)
    group = lane >> 3
    sigma = jnp.where(
        group == 0, SHIFTS[0], jnp.where(group == 1, SHIFTS[1], jnp.where(group == 2, SHIFTS[2], SHIFTS[3]))
    )
    moment = jnp.where(lane < 32, sigma * gram + SCALE * pltpu.roll(gram, NZ - 8, 1), 0.0)
    flipped = jnp.transpose(jnp.concatenate([moment, jnp.zeros((NZ - 32, NZ), F32)], 0))[:32]
    moment = 0.5 * (moment + flipped)
    left = jnp.where(lane < 32, gram, jnp.where(lane == row + 32, 1.0, 0.0))
    right = jnp.where(lane < 32, moment, jnp.where(group == 4, pltpu.roll(gram, 32, 1), 0.0))
    inverse = jnp.zeros((32, NZ), F32)
    for j in range(0, 32, 2):
        kept = []
        for matrix in (left, right):
            c0 = jnp.broadcast_to(matrix[:, j : j + 1], (32, NZ))
            c1 = jnp.broadcast_to(matrix[:, j + 1 : j + 2], (32, NZ))
            r0, r1 = matrix[j : j + 1], matrix[j + 1 : j + 2]
            p, q, r = c0[j : j + 1], c1[j : j + 1], c1[j + 1 : j + 2]
            inv = 1.0 / (p * r - q * q)
            n0, n1 = (r * r0 - q * r1) * inv, (p * r1 - q * r0) * inv
            kept.append((matrix - c0 * n0 - c1 * n1, r0, r1, p, q, r, n0, n1))
        left, r0, r1, p, q, r, _, _ = kept[0]
        ratio = q / p
        inverse = jnp.where(row == j, r0 * lax.rsqrt(p), inverse)
        inverse = jnp.where(row == j + 1, (r1 - ratio * r0) * lax.rsqrt(r - q * ratio), inverse)
        right, n0, n1 = kept[1][0], kept[1][6], kept[1][7]
        right = jnp.where(row == j, n0, jnp.where(row == j + 1, n1, right))
    inverse = pltpu.roll(inverse, NZ - 32, 1)
    coeff = pltpu.roll(right, NZ - 32, 1)
    coeff = jnp.transpose(jnp.concatenate([coeff, jnp.zeros((NZ - 32, NZ), F32)], 0))[:8]
    coeff = jnp.where(lane8 < S, coeff, 0.0)
    ext = SCALE * pltpu.roll(coeff, 8, 1)
    for k in range(S):
        ext = jnp.where(lane8 == k, ext + SHIFTS[k] * coeff, ext)
    full = jnp.concatenate([jnp.where(lane < 32, inverse, 0.0), coeff, ext], 0)
    lanes = lane_ids((48, NZ))
    spread = jnp.zeros((48, NZ), F32)
    for k in range(S + 1):
        for part in range(2):
            spread = jnp.where(
                (lanes >> 3) == 2 * k + part, pltpu.roll(full, (8 * (2 * k + part - k)) % NZ, 1), spread
            )
    high = spread.astype(BF16)
    low = (spread - high.astype(F32)).astype(BF16)
    weight[0:48] = high
    weight[48:96] = low


def finish_kernel(packed, s0, s1, s2, s3, s4, sol, v0, new_sol, new_res, basis, weight):
    c = pl.program_id(0)

    @pl.when(c == 0)
    def _():
        total = packed[0]
        for i in range(1, packed.shape[0]):
            total = total + packed[i]
        factor(total, weight)

    def loop(i, _):
        spots = [(4 * i + u, y) for u in range(4) for y in range(NY)]
        lines = [jnp.concatenate([s[c, x, y] for x, y in spots], 1) for s in (s0, s1, s2, s3, s4)]
        stack = jnp.concatenate(lines, 0)
        both = jnp.dot(weight[:, 0:80], stack, preferred_element_type=F32)
        both = both[0:48] + both[48:96]
        for number, (x, y) in enumerate(spots):
            part = both[:, number * NZ : (number + 1) * NZ]
            for q in range(4):
                basis[pl.ds(512 * q + x * 8 + y, 8, stride=64), :] = part[8 * q : 8 * q + 8]
            spot = pl.ds(x * 8 + y, 8, stride=64)
            new_sol[spot, :] = sol[pl.ds(c * 512 + x * 8 + y, 8, stride=64), :] + part[32:40]
            new_res[spot, :] = v0[c, x, y] - part[40:48]
        return 0

    lax.fori_loop(0, 2, loop, 0)


def shaped(*shape, dtype=F32):
    return jax.ShapeDtypeStruct(shape, dtype)


def near(*shape, dtype=F32):
    return pltpu.VMEM(shape, dtype)


def far(array):
    return pltpu.with_memory_space_constraint(array, pltpu.HBM)


def params(mib):
    return pltpu.CompilerParams(vmem_limit_bytes=mib << 20)


def exchange(sends):
    moved = []
    for number, (axis, up) in enumerate((("gx", 1), ("gx", 0), ("gy", 1), ("gy", 0), ("gz", 1), ("gz", 0))):
        count = lax.axis_size(axis)
        if up:
            links = [(i, (i + 1) % count) for i in range(count)]
        else:
            links = [((i + 1) % count, i) for i in range(count)]
        if axis == "gz":
            source = sends[4]
        else:
            source = sends[number + 1 if up else number - 1]
        moved.append(lax.ppermute(source, axis, links))
    return moved


def body(solution, residual, permeability, storage, tissue_mask, tissue_label, exchange_table):
    flat = residual.reshape(-1, NZ)
    edge = []
    for axis in ("gx", "gy", "gz"):
        place = lax.axis_index(axis)
        edge += [place > 0, place < lax.axis_size(axis) - 1]
    edge = jnp.stack(edge).astype(jnp.int32)
    field = near(COMP, NX, NY, RHS, NZ)
    face = near(FACE + 5, 8, NZ)
    total = COMP * RHS * NX * NY
    in_hbm = pl.BlockSpec(memory_space=pltpu.HBM)
    v0, *sends, inner = pl.pallas_call(
        pack_kernel,
        out_shape=(field, face, face, face, face, face, near(5, NX, NY, NZ)),
        in_specs=[SMEM] + [in_hbm] * 3,
        out_specs=[VMEM] * 7,
        scratch_shapes=[
            pltpu.VMEM((total, NZ), F32),
            pltpu.VMEM((NX, NY, NZ), jnp.int32),
            pltpu.SemaphoreType.DMA((3,)),
        ],
        compiler_params=params(5),
        name="pack",
    )(edge, far(flat), far(permeability), far(tissue_mask))

    wide, tall = lax.axis_size("gx") * lax.axis_size("gz"), lax.axis_size("gy")

    def gram(index, current, older, before):
        inputs = [current, *older, *before]
        return pl.pallas_call(
            lambda *refs: gram_kernel(index, *refs),
            out_shape=(
                near(COMP, NX, NY, 16, NZ, dtype=BF16),
                near(8, NZ) if index < S else near(wide, 8, NZ),
            ),
            in_specs=[VMEM] * len(inputs),
            out_specs=[VMEM] * 2,
            compiler_params=params(5),
            cost_estimate=pl.CostEstimate(
                flops=2 * 16 * 16 * (index + 1) * 32768, bytes_accessed=(3 + index) << 20, transcendentals=0
            ),
            name=f"gram{index}",
        )(*inputs)

    halo = exchange(sends)
    splits = []
    sol, rate, base = pl.pallas_call(
        prepare_kernel,
        out_shape=(near(total, NZ), near(6, NX, NY, NZ), near(COMP, NX, NY, NZ)),
        in_specs=[SMEM, VMEM] + [in_hbm] * 3,
        out_specs=[VMEM] * 3,
        scratch_shapes=[pltpu.VMEM((NX, NY, NZ), jnp.int32), pltpu.SemaphoreType.DMA((3,))],
        compiler_params=params(5),
        name="prepare",
    )(exchange_table, inner, far(solution.reshape(total, NZ)), far(storage), far(tissue_label))
    split, piece = gram(0, v0, [], [])
    splits.append(split)
    face = near(FACE, 8, NZ)
    side_outs = [face] * 5
    coef_shapes = [
        near(COMP, NX + 1, NY, NZ),
        near(2 * COMP, NX, NY, NZ),
        near(2 * COMP, NX, NY, NZ),
        near(COMP, NX, NY, NZ),
    ]
    work = [pltpu.VMEM((COMP, NX + 2, NY, RHS, NZ), F32), pltpu.VMEM((COMP, 8, NZ), F32)]
    results = pl.pallas_call(
        first_kernel,
        out_shape=[field] + side_outs + coef_shapes,
        in_specs=[SMEM] + [VMEM] * 11,
        out_specs=[VMEM] * 10,
        scratch_shapes=work + [pltpu.VMEM((5, NX + 2, NY, NZ), F32), pltpu.VMEM((5, 8, NZ), F32)],
        compiler_params=params(8),
        name="step1",
    )(edge, piece, v0, inner, base, rate, *halo)
    current, sends, coef = results[0], results[1:6], list(results[6:10]) + [rate]
    for index in range(1, S):
        halo = exchange(sends)
        split, piece = gram(index, current, splits, [piece])
        splits.append(split)
        outs = [field] + (side_outs if index < S - 1 else [])
        results = pl.pallas_call(
            lambda *refs, index=index: step_kernel(index, *refs),
            out_shape=outs,
            in_specs=[VMEM] * 13,
            out_specs=[VMEM] * len(outs),
            scratch_shapes=work,
            compiler_params=params(6),
            name=f"step{index + 1}",
        )(piece, current, *halo, *coef)
        current, sends = results[0], results[1:]
    split, piece = gram(S, current, splits, [piece])
    splits.append(split)
    parts = lax.all_to_all(piece, ("gx", "gz"), 0, 0)
    parts = pl.pallas_call(
        relay_kernel,
        out_shape=near(tall, 8, NZ),
        in_specs=[VMEM],
        out_specs=VMEM,
        compiler_params=params(2),
        name="relay",
    )(parts)
    packed = lax.all_to_all(parts, ("gy",), 0, 0)
    rows = pl.BlockSpec((RHS * NX * NY, NZ), lambda c: (c, 0))
    new_sol, new_res, basis = pl.pallas_call(
        finish_kernel,
        grid=(COMP,),
        out_shape=(shaped(total, NZ), shaped(total, NZ), shaped(total * S, NZ)),
        in_specs=[VMEM] * 8,
        out_specs=(rows, rows, pl.BlockSpec((S * RHS * NX * NY, NZ), lambda c: (c, 0))),
        scratch_shapes=[pltpu.VMEM((96, NZ), BF16)],
        compiler_params=params(14),
        name="finish",
    )(packed, *splits, sol, v0)
    return (
        new_sol.reshape(solution.shape),
        new_res.reshape(residual.shape),
        basis.reshape((COMP, S * RHS) + solution.shape[2:]),
    )


def solution(mesh):
    wide = P(None, None, "gx", "gy", "gz")
    return jax.shard_map(
        body,
        mesh=mesh,
        in_specs=(
            wide,
            wide,
            P(None, "gx", "gy", "gz"),
            P(None, "gx", "gy", "gz"),
            P("gx", "gy", "gz"),
            P("gx", "gy", "gz"),
            P(),
        ),
        out_specs=(wide, wide, wide),
        check_vma=False,
    )
```

```python
import jax
import jax.numpy as jnp
from jax import lax
from jax.experimental import pallas as pl
from jax.experimental.pallas import tpu as pltpu
from jax.sharding import PartitionSpec as P

COMP = 4
RHS = 8
S = 4
PAIRS = ((0, 1), (0, 2), (0, 3), (1, 2), (1, 3), (2, 3))
SHIFTS = (2.0, 14.0, 6.0, 10.0)
SCALE = 8.0
F32 = jnp.float32
BF16 = jnp.bfloat16

PITCH = 72
NX, NY, NZ = 8, 8, 128
FACE = COMP * 8
BLOCKS = tuple((a, b) for b in range(4) for a in range(b + 1)) + ((3, 4),)
VMEM = pl.BlockSpec(memory_space=pltpu.VMEM)
SMEM = pl.BlockSpec(memory_space=pltpu.SMEM)


def pair_index(a, b):
    return PAIRS.index((min(a, b), max(a, b)))


def lane_ids(shape):
    return lax.broadcasted_iota(jnp.int32, shape, len(shape) - 1)


def put_ends(acc, tile, lane, slot):
    return jnp.where((lane >> 1) == slot, pltpu.roll(tile, 2 * slot + 1, 1), acc)


def join(lines, lane):
    while len(lines) > 1:
        half = 128 // len(lines)
        lines = [
            jnp.where((lane & half) == 0, low, high) for low, high in zip(lines[::2], lines[1::2])
        ]
    return lines[0]


def fetch(pairs, sems):
    copies = [pltpu.make_async_copy(src, dst, sems.at[i]) for i, (src, dst) in enumerate(pairs)]
    for copy in copies:
        copy.start()
    return copies


def pack_kernel(edge, res_hbm, perm_hbm, mask_hbm, v0, xlo, xhi, ylo, yhi, ends, pm, res, mask, sems):
    lane = lane_ids((8, NZ))
    spaced = res.reshape(COMP * RHS, PITCH, NZ)
    spans = [pl.ds(RHS * c, RHS) for c in range(COMP)]
    copies = fetch(
        [(perm_hbm, pm.at[pl.ds(0, COMP)]), (mask_hbm, mask)]
        + [(res_hbm.at[span], spaced.at[span, pl.ds(0, NX * NY)]) for span in spans],
        sems,
    )
    copies[0].wait()
    copies[1].wait()

    for x in range(NX):
        pm[COMP, x] = mask[x].astype(F32)
    for f in range(5):
        acc = jnp.zeros((8, NZ), F32)
        for x in range(NX):
            tile = pm[f, x]
            ylo[FACE + f, x : x + 1, :] = tile[0:1]
            yhi[FACE + f, x : x + 1, :] = tile[7:8]
            acc = put_ends(acc, tile, lane, x)
        ends[COMP + f] = acc
    for f in range(5):
        xlo[FACE + f] = pm[f, 0]
        xhi[FACE + f] = pm[f, NX - 1]

    for c in range(COMP):
        copies[2 + c].wait()
        lines = []
        for x in range(NX):
            acc = jnp.zeros((8, NZ), F32)
            for y in range(NY):
                tile = res[pl.ds(c * RHS * PITCH + x * 8 + y, 8, stride=PITCH), :]
                v0[c, x, y] = tile
                acc = put_ends(acc, tile, lane, x * 8 + y)
                if y in (0, NY - 1):
                    (yhi if y else ylo)[c * 8 + x] = tile
                if x in (0, NX - 1):
                    (xhi if x else xlo)[c * 8 + y] = tile
            lines.append(acc)
        ends[c] = join(lines, lane)


def face(own, other, masks):
    return (-0.5 / SCALE) * (own + other) * masks


def prepare_kernel(table, pm, sol_hbm, store_hbm, label_hbm, sol, tx, ty, tz, diag, rate, label, sems):
    lane = lane_ids((8, NZ))
    sub = lax.broadcasted_iota(jnp.int32, (8, NZ), 0)
    copies = fetch([(store_hbm, diag), (label_hbm, label), (sol_hbm, sol)], sems)
    copies[0].wait()
    copies[1].wait()

    for x in range(NX):
        m = pm[COMP, x]
        kind = label[x]
        rates = []
        for q in range(6):
            value = jnp.where(kind == 0, table[0, q], jnp.where(kind == 1, table[1, q], table[2, q]))
            rates.append((1.0 / SCALE) * m * value)
            rate[q, x] = rates[q]
        below, above = max(x - 1, 0), min(x + 1, NX - 1)
        m_lo = m * pm[COMP, below] if x else jnp.zeros_like(m)
        m_hi = m * pm[COMP, above] if x < NX - 1 else jnp.zeros_like(m)

        def around(own):
            return [pltpu.roll(own, 1, 0), pltpu.roll(own, 7, 0), pltpu.roll(own, 1, 1), pltpu.roll(own, 127, 1)]

        outer = [sub == 0, sub == 7, lane == 0, lane == 127]
        masks = [jnp.where(edge, 0.0, m * n) for edge, n in zip(outer, around(m))]
        for c in range(COMP):
            own = pm[c, x]
            total = diag[c, x] * (1.0 / SCALE)
            for b in range(COMP):
                if b != c:
                    total = total + rates[pair_index(c, b)]
            tx[c, x] = x_lo = face(own, pm[c, below], m_lo)
            tx[COMP + c, x] = x_hi = face(own, pm[c, above], m_hi)
            sides = [face(own, n, mm) for n, mm in zip(around(own), masks)]
            ty[c, x], ty[COMP + c, x], tz[c, x], tz[COMP + c, x] = sides
            diag[c, x] = total - x_lo - x_hi - sides[0] - sides[1] - sides[2] - sides[3]
    copies[2].wait()


def local_kernel(index, cur, tx, ty, tz, diag, rate, out):
    shift = SHIFTS[index] / SCALE

    def loop(x, _):
        below, above = jnp.maximum(x - 1, 0), jnp.minimum(x + 1, NX - 1)
        low = None
        own = [cur[c, x, 0] for c in range(COMP)]
        for y in range(NY):
            row = pl.ds(y, 1)
            high = [cur[c, x, y + 1] for c in range(COMP)] if y < NY - 1 else None
            rates = [rate[q, x, row, :] for q in range(6)]
            for c in range(COMP):
                p = own[c]
                value = (diag[c, x, row, :] - shift) * p
                side = tx[c, x, row, :] * cur[c, below, y] + tx[COMP + c, x, row, :] * cur[c, above, y]
                if y:
                    value = value + ty[c, x, row, :] * low[c]
                if y < NY - 1:
                    side = side + ty[COMP + c, x, row, :] * high[c]
                value = value + tz[c, x, row, :] * pltpu.roll(p, 1, 1)
                side = side + tz[COMP + c, x, row, :] * pltpu.roll(p, 127, 1)
                others = [b for b in range(COMP) if b != c]
                flow = rates[pair_index(c, others[0])] * own[others[0]]
                for b in others[1:]:
                    flow = flow + rates[pair_index(c, b)] * own[b]
                out[c, x, y] = (value + side) - flow
            low, own = own, high
        return 0

    lax.fori_loop(0, NX, loop, 0)


def ghost_tile(place, first, second, lane):
    return jnp.where(((lane + place[6]) & 1) == 0, second, first)


def edge_kernel(place, inner, halo, bx, by, bz):
    xl, xh, yl, yh, z0, z1 = halo
    lane = lane_ids((8, NZ))
    keep = [place[i].astype(F32) for i in range(6)]
    tiles = [ghost_tile(place, z0[COMP + f], z1[COMP + f], lane) for f in range(5)]
    tiles[4] = tiles[4] * jnp.where((lane & 1) == 0, keep[4], keep[5])
    for side, (halo_x, halo_y) in enumerate(((xl, yl), (xh, yh))):
        x = side * (NX - 1)
        mask = inner[COMP, x] * halo_x[FACE + COMP] * keep[side]
        for c in range(COMP):
            bx[side, c] = face(inner[c, x], halo_x[FACE + c], mask)

    for x in range(NX):
        row = pl.ds(x, 1)
        for side, halo_y in enumerate((yl, yh)):
            own = pl.ds(side * (NY - 1), 1)
            mask = inner[COMP, x, own, :] * halo_y[FACE + COMP, row, :] * keep[2 + side]
            for c in range(COMP):
                by[side, c, row, :] = face(inner[c, x, own, :], halo_y[FACE + c, row, :], mask)
        near_x = [pltpu.roll(t, (128 - 2 * x) & 127, 1) for t in tiles]
        ghosts = [jnp.where(lane == 0, t, pltpu.roll(t, 126, 1)) for t in near_x]
        mask = jnp.where((lane == 0) | (lane == 127), inner[COMP, x] * ghosts[4], 0.0)
        for c in range(COMP):
            bz[c, x] = face(inner[c, x], ghosts[c], mask)


def close_step(place, part, cur, halo, bx, by, bz, out, sends):
    xl, xh, yl, yh, z0, z1 = halo
    lane = lane_ids((8, NZ))
    ghosts, lines = [], [[] for _ in range(COMP)]
    for c in range(COMP):
        tile = ghost_tile(place, z0[c], z1[c], lane)
        ghosts.append(jnp.where((lane & 1) == 0, pltpu.roll(tile, 127, 1), pltpu.roll(tile, 1, 1)))
    for x in range(NX):
        accs = [jnp.zeros((8, NZ), F32) for _ in range(COMP)]
        for y in range(NY):
            slot = x * 8 + y
            for c in range(COMP):
                p = cur[c, x, y]
                g = pltpu.roll(ghosts[c], (127 - 2 * slot) & 127, 1)
                value = part[c, x, y] + bz[c, x, pl.ds(y, 1), :] * (g - p)
                if y in (0, NY - 1):
                    side = 1 if y else 0
                    other = (yl, yh)[side][c * 8 + x]
                    value = value + by[side, c, pl.ds(x, 1), :] * (other - p)
                if x in (0, NX - 1):
                    side = 1 if x else 0
                    other = (xl, xh)[side][c * 8 + y]
                    value = value + bx[side, c, pl.ds(y, 1), :] * (other - p)
                out[c, x, y] = value
                if sends is not None:
                    accs[c] = put_ends(accs[c], value, lane, slot)
                    if y in (0, NY - 1):
                        sends[2 + (1 if y else 0)][c * 8 + x] = value
                    if x in (0, NX - 1):
                        sends[1 if x else 0][c * 8 + y] = value
        for c in range(COMP):
            lines[c].append(accs[c])
    if sends is not None:
        for c in range(COMP):
            sends[4][c] = join(lines[c], lane)


def first_kernel(place, part, cur, inner, *refs):
    halo, refs = refs[:6], refs[6:]
    out, sends, faces = refs[0], refs[1:6], refs[6:9]
    edge_kernel(place, inner, halo, *faces)
    close_step(place, part, cur, halo, *faces, out, sends)


def step_kernel(place, piece, part, cur, *refs):
    halo, faces, refs = refs[:6], refs[6:9], refs[9:]
    out, sends = refs[0], refs[1:] or None
    close_step(place, part, cur, halo, *faces, out, sends)


def gram_kernel(index, cur, *refs):
    others = [a for a, b in BLOCKS if b == index]
    count = len(others)
    older, refs = refs[: count - (index < S)], refs[count - (index < S) :]
    before = None
    if index:
        before, refs = refs[0], refs[1:]
    split, out = refs
    lane = lane_ids((8, NZ))
    tall = 16 * count

    def loop(x, total):
        tiles = []
        for c in range(COMP):
            for y in range(NY):
                v = cur[c, x, y]
                high = v.astype(BF16).astype(F32)
                tile = jnp.concatenate([high, v - high], 0).astype(BF16)
                split[c, x, y] = tile
                tiles.append(tile)
        right = jnp.concatenate(tiles, 1)
        lefts = [
            jnp.concatenate([old[c, x, y] for c in range(COMP) for y in range(NY)], 1) for old in older
        ]
        if index < S:
            lefts.append(right)
        left = jnp.concatenate(lefts, 0) if len(lefts) > 1 else lefts[0]
        return total + lax.dot_general(
            left, right, (((1,), (1,)), ((), ())), preferred_element_type=F32
        )

    total = lax.fori_loop(0, NX, loop, jnp.zeros((tall, 16), F32))
    wide = jnp.concatenate([total, jnp.zeros((tall, NZ - 16), F32)], 1)
    value = jnp.zeros((8, NZ), F32)
    for number, a in enumerate(others):
        top = 16 * number
        both = wide[top : top + 8] + wide[top + 8 : top + 16]
        both = both + pltpu.roll(both, NZ - 8, 1)
        slot = BLOCKS.index((a, index))
        value = jnp.where((lane >> 3) == slot, pltpu.roll(both, 8 * slot, 1), value)
    if index:
        value = value + before[...]
    if index < S:
        out[...] = value
    else:
        for copy in range(out.shape[0]):
            out[copy] = value


def relay_kernel(parts, out):
    total = parts[0]
    for i in range(1, parts.shape[0]):
        total = total + parts[i]
    for copy in range(out.shape[0]):
        out[copy] = total


def lane_group(tile, source, target):
    return pltpu.roll(tile, (8 * (target - source)) % NZ, 1)


def factor(packed, weight):
    lane8 = lane_ids((8, NZ)) >> 3
    turned = jnp.transpose(jnp.concatenate([packed, jnp.zeros((NZ - 8, NZ), F32)], 0))
    rows = []
    for a in range(S):
        line = jnp.zeros((8, NZ), F32)
        for b in range(S + 1):
            if b == S and a < S - 1:
                block = lane_group(packed, BLOCKS.index((a + 1, 3)), b)
                block = block + (SHIFTS[a] - SHIFTS[3]) / SCALE * lane_group(
                    packed, BLOCKS.index((a, 3)), b
                )
            elif a <= b:
                block = lane_group(packed, BLOCKS.index((a, b)), b)
            else:
                slot = BLOCKS.index((b, a))
                block = lane_group(turned[8 * slot : 8 * slot + 8], 0, b)
            if a == b:
                slot = BLOCKS.index((a, a))
                other = lane_group(turned[8 * slot : 8 * slot + 8], 0, b)
                block = 0.5 * (block + other)
            line = jnp.where(lane8 == b, block, line)
        rows.append(line)
    gram = jnp.concatenate(rows, 0)
    lane = lane_ids((32, NZ))
    row = lax.broadcasted_iota(jnp.int32, (32, NZ), 0)
    group = lane >> 3
    sigma = jnp.where(
        group == 0, SHIFTS[0], jnp.where(group == 1, SHIFTS[1], jnp.where(group == 2, SHIFTS[2], SHIFTS[3]))
    )
    moment = jnp.where(lane < 32, sigma * gram + SCALE * pltpu.roll(gram, NZ - 8, 1), 0.0)
    flipped = jnp.transpose(jnp.concatenate([moment, jnp.zeros((NZ - 32, NZ), F32)], 0))[:32]
    moment = 0.5 * (moment + flipped)
    left = jnp.where(lane < 32, gram, jnp.where(lane == row + 32, 1.0, 0.0))
    right = jnp.where(lane < 32, moment, jnp.where(group == 4, pltpu.roll(gram, 32, 1), 0.0))
    inverse = jnp.zeros((32, NZ), F32)
    for j in range(0, 32, 2):
        kept = []
        for matrix in (left, right):
            c0 = jnp.broadcast_to(matrix[:, j : j + 1], (32, NZ))
            c1 = jnp.broadcast_to(matrix[:, j + 1 : j + 2], (32, NZ))
            r0, r1 = matrix[j : j + 1], matrix[j + 1 : j + 2]
            p, q, r = c0[j : j + 1], c1[j : j + 1], c1[j + 1 : j + 2]
            inv = 1.0 / (p * r - q * q)
            n0, n1 = (r * r0 - q * r1) * inv, (p * r1 - q * r0) * inv
            kept.append((matrix - c0 * n0 - c1 * n1, r0, r1, p, q, r, n0, n1))
        left, r0, r1, p, q, r, _, _ = kept[0]
        ratio = q / p
        inverse = jnp.where(row == j, r0 * lax.rsqrt(p), inverse)
        inverse = jnp.where(row == j + 1, (r1 - ratio * r0) * lax.rsqrt(r - q * ratio), inverse)
        right, n0, n1 = kept[1][0], kept[1][6], kept[1][7]
        right = jnp.where(row == j, n0, jnp.where(row == j + 1, n1, right))
    inverse = pltpu.roll(inverse, NZ - 32, 1)
    coeff = pltpu.roll(right, NZ - 32, 1)
    coeff = jnp.transpose(jnp.concatenate([coeff, jnp.zeros((NZ - 32, NZ), F32)], 0))[:8]
    coeff = jnp.where(lane8 < S, coeff, 0.0)
    ext = SCALE * pltpu.roll(coeff, 8, 1)
    for k in range(S):
        ext = jnp.where(lane8 == k, ext + SHIFTS[k] * coeff, ext)
    full = jnp.concatenate([jnp.where(lane < 32, inverse, 0.0), coeff, ext], 0)
    lanes = lane_ids((48, NZ))
    spread = jnp.zeros((48, NZ), F32)
    for k in range(S + 1):
        for part in range(2):
            spread = jnp.where(
                (lanes >> 3) == 2 * k + part, pltpu.roll(full, (8 * (2 * k + part - k)) % NZ, 1), spread
            )
    high = spread.astype(BF16)
    low = (spread - high.astype(F32)).astype(BF16)
    weight[0:48] = high
    weight[48:96] = low


def finish_kernel(packed, s0, s1, s2, s3, s4, sol, v0, sol_hbm, res_hbm, basis_hbm, new_sol, new_res, basis, weight, sems):
    total = packed[0]
    for i in range(1, packed.shape[0]):
        total = total + packed[i]
    factor(total, weight)
    copies = []
    for c in range(COMP):
        for half in range(2):
            spots = [(4 * half + u, y) for u in range(4) for y in range(NY)]
            lines = [jnp.concatenate([s[c, x, y] for x, y in spots], 1) for s in (s0, s1, s2, s3, s4)]
            both = jnp.dot(weight[:, 0:80], jnp.concatenate(lines, 0), preferred_element_type=F32)
            both = both[0:48] + both[48:96]
            for number, (x, y) in enumerate(spots):
                place = x * 8 + y
                part = both[:, number * NZ : (number + 1) * NZ]
                for q in range(0, S * RHS, 8):
                    first = (c * S * RHS + q) * PITCH + place
                    basis[pl.ds(first, 8, stride=PITCH), :] = part[q : q + 8]
                spot = pl.ds(c * RHS * PITCH + place, 8, stride=PITCH)
                old = sol[pl.ds(c * RHS * NX * NY + place, 8, stride=NX * NY), :]
                new_sol[spot, :] = old + part[32:40]
                new_res[spot, :] = v0[c, x, y] - part[40:48]
        pieces = ((basis, basis_hbm, S * RHS), (new_sol, sol_hbm, RHS), (new_res, res_hbm, RHS))
        for number, (source, target, count) in enumerate(pieces):
            spaced = source.reshape(source.shape[0] // PITCH, PITCH, NZ)
            span = pl.ds(c * count, count)
            copies.append(
                pltpu.make_async_copy(
                    spaced.at[span, pl.ds(0, NX * NY)], target.at[span], sems.at[c, number]
                )
            )
            copies[-1].start()
    for copy in copies:
        copy.wait()


def shaped(*shape, dtype=F32):
    return jax.ShapeDtypeStruct(shape, dtype)


def near(*shape, dtype=F32):
    return pltpu.VMEM(shape, dtype)


def far(array):
    return pltpu.with_memory_space_constraint(array, pltpu.HBM)


def params(mib):
    return pltpu.CompilerParams(vmem_limit_bytes=mib << 20)


def exchange(sends):
    moved = []
    for number, (axis, up) in enumerate((("gx", 1), ("gx", 0), ("gy", 1), ("gy", 0))):
        count = lax.axis_size(axis)
        if up:
            links = [(i, (i + 1) % count) for i in range(count)]
        else:
            links = [((i + 1) % count, i) for i in range(count)]
        moved.append(lax.ppermute(sends[number + 1 if up else number - 1], axis, links))
    count = lax.axis_size("gz")
    moved.append(lax.ppermute(sends[4], "gz", [(i, i ^ 1) for i in range(count)]))
    links = [(i, (i + (1 if i % 2 else -1)) % count) for i in range(count)]
    moved.append(lax.ppermute(sends[4], "gz", links))
    return moved


def body(solution, residual, permeability, storage, tissue_mask, tissue_label, exchange_table):
    flat = residual.reshape(COMP * RHS, NX * NY, NZ)
    edge = []
    for axis in ("gx", "gy", "gz"):
        place = lax.axis_index(axis)
        edge += [place > 0, place < lax.axis_size(axis) - 1]
    edge.append(place % 2 == 1)
    edge = jnp.stack(edge).astype(jnp.int32)
    field = near(COMP, NX, NY, RHS, NZ)
    face = near(FACE + 5, 8, NZ)
    total = COMP * RHS * NX * NY
    in_hbm = pl.BlockSpec(memory_space=pltpu.HBM)
    v0, *sends, inner = pl.pallas_call(
        pack_kernel,
        out_shape=(field, face, face, face, face, face, near(5, NX, NY, NZ)),
        in_specs=[SMEM] + [in_hbm] * 3,
        out_specs=[VMEM] * 7,
        scratch_shapes=[
            pltpu.VMEM((COMP * RHS * PITCH, NZ), F32),
            pltpu.VMEM((NX, NY, NZ), jnp.int32),
            pltpu.SemaphoreType.DMA((2 + COMP,)),
        ],
        compiler_params=params(5),
        name="pack",
    )(edge, far(flat), far(permeability), far(tissue_mask))

    wide, tall = lax.axis_size("gx") * lax.axis_size("gz"), lax.axis_size("gy")

    def gram(index, current, older, before):
        inputs = [current, *(older if index < S else older[-1:]), *before]
        return pl.pallas_call(
            lambda *refs: gram_kernel(index, *refs),
            out_shape=(
                near(COMP, NX, NY, 16, NZ, dtype=BF16),
                near(8, NZ) if index < S else near(wide, 8, NZ),
            ),
            in_specs=[VMEM] * len(inputs),
            out_specs=[VMEM] * 2,
            compiler_params=params(5),
            cost_estimate=pl.CostEstimate(
                flops=2 * 16 * 16 * (index + 1) * 32768, bytes_accessed=(3 + index) << 20, transcendentals=0
            ),
            name=f"gram{index}",
        )(*inputs)

    halo = exchange(sends)
    splits = []
    plane = near(COMP, NX, NY, NZ)
    double = near(2 * COMP, NX, NY, NZ)
    sol, *coef = pl.pallas_call(
        prepare_kernel,
        out_shape=(near(total, NZ), double, double, double, plane, near(6, NX, NY, NZ)),
        in_specs=[SMEM, VMEM] + [in_hbm] * 3,
        out_specs=[VMEM] * 6,
        scratch_shapes=[pltpu.VMEM((NX, NY, NZ), jnp.int32), pltpu.SemaphoreType.DMA((3,))],
        compiler_params=params(5),
        name="prepare",
    )(exchange_table, inner, far(solution.reshape(total, NZ)), far(storage), far(tissue_label))

    def local(index, current):
        return pl.pallas_call(
            lambda *refs: local_kernel(index, *refs),
            out_shape=field,
            in_specs=[VMEM] * 6,
            out_specs=VMEM,
            compiler_params=params(5),
            cost_estimate=pl.CostEstimate(flops=6 << 20, bytes_accessed=3 << 20, transcendentals=0),
            name=f"local{index + 1}",
        )(current, *coef)

    part = local(0, v0)
    split, piece = gram(0, v0, [], [])
    splits.append(split)
    face = near(FACE, 8, NZ)
    results = pl.pallas_call(
        first_kernel,
        out_shape=[field] + [face] * 5 + [near(2, COMP, NY, NZ), near(2, COMP, NX, NZ), plane],
        in_specs=[SMEM] + [VMEM] * 9,
        out_specs=[VMEM] * 9,
        compiler_params=params(5),
        name="step1",
    )(edge, part, v0, inner, *halo)
    current, sends, faces = results[0], results[1:6], results[6:]
    for index in range(1, S):
        halo = exchange(sends)
        part = local(index, current)
        split, piece = gram(index, current, splits, [piece])
        splits.append(split)
        outs = [field] + ([face] * 5 if index < S - 1 else [])
        results = pl.pallas_call(
            step_kernel,
            out_shape=outs,
            in_specs=[SMEM] + [VMEM] * 12,
            out_specs=[VMEM] * len(outs),
                compiler_params=params(5),
            name=f"step{index + 1}",
        )(edge, piece, part, current, *halo, *faces)
        current, sends = results[0], results[1:]
    split, piece = gram(S, current, splits, [piece])
    splits.append(split)
    parts = lax.all_to_all(piece, ("gx", "gz"), 0, 0)
    parts = pl.pallas_call(
        relay_kernel,
        out_shape=near(tall, 8, NZ),
        in_specs=[VMEM],
        out_specs=VMEM,
        compiler_params=params(2),
        name="relay",
    )(parts)
    packed = lax.all_to_all(parts, ("gy",), 0, 0)
    count = COMP * RHS
    new_sol, new_res, basis = pl.pallas_call(
        finish_kernel,
        out_shape=(shaped(count, NX * NY, NZ), shaped(count, NX * NY, NZ), shaped(S * count, NX * NY, NZ)),
        in_specs=[VMEM] * 8,
        out_specs=[in_hbm] * 3,
        scratch_shapes=[
            pltpu.VMEM((count * PITCH, NZ), F32),
            pltpu.VMEM((count * PITCH, NZ), F32),
            pltpu.VMEM((S * count * PITCH, NZ), F32),
            pltpu.VMEM((96, NZ), BF16),
            pltpu.SemaphoreType.DMA((COMP, 3)),
        ],
        compiler_params=params(24),
        name="finish",
    )(packed, *splits, sol, v0)
    return (
        new_sol.reshape(solution.shape),
        new_res.reshape(residual.shape),
        basis.reshape((COMP, S * RHS) + solution.shape[2:]),
    )


def solution(mesh):
    wide = P(None, None, "gx", "gy", "gz")
    return jax.shard_map(
        body,
        mesh=mesh,
        in_specs=(
            wide,
            wide,
            P(None, "gx", "gy", "gz"),
            P(None, "gx", "gy", "gz"),
            P("gx", "gy", "gz"),
            P("gx", "gy", "gz"),
            P(),
        ),
        out_specs=(wide, wide, wide),
        check_vma=False,
    )
```

```python
import jax
import jax.numpy as jnp
from jax import lax
from jax.experimental import pallas as pl
from jax.experimental.pallas import tpu as pltpu
from jax.sharding import PartitionSpec as P

COMP = 4
RHS = 8
S = 4
PAIRS = ((0, 1), (0, 2), (0, 3), (1, 2), (1, 3), (2, 3))
SHIFTS = (2.0, 14.0, 6.0, 10.0)
SCALE = 8.0
F32 = jnp.float32
BF16 = jnp.bfloat16

PITCH = 72
NX, NY, NZ = 8, 8, 128
FACE = COMP * 8
BLOCKS = tuple((a, b) for b in range(4) for a in range(b + 1)) + ((3, 4),)
VMEM = pl.BlockSpec(memory_space=pltpu.VMEM)
SMEM = pl.BlockSpec(memory_space=pltpu.SMEM)


def pair_index(a, b):
    return PAIRS.index((min(a, b), max(a, b)))


def lane_ids(shape):
    return lax.broadcasted_iota(jnp.int32, shape, len(shape) - 1)


def put_ends(acc, tile, lane, slot):
    return jnp.where((lane >> 1) == slot, pltpu.roll(tile, 2 * slot + 1, 1), acc)


def chooser(place, axis):
    odd = (jnp.zeros((8, NZ), jnp.int32) + place[6 + axis]) == 1

    def pick(side, first, second):
        mask = odd[: first.shape[0]]
        return jnp.where(mask, second, first) if side else jnp.where(mask, first, second)

    return pick


def join(lines, lane):
    while len(lines) > 1:
        half = 128 // len(lines)
        lines = [
            jnp.where((lane & half) == 0, low, high) for low, high in zip(lines[::2], lines[1::2])
        ]
    return lines[0]


def fetch(pairs, sems):
    copies = [pltpu.make_async_copy(src, dst, sems.at[i]) for i, (src, dst) in enumerate(pairs)]
    for copy in copies:
        copy.start()
    return copies


def pack_kernel(place, res_hbm, perm_hbm, mask_hbm, v0, xa, xb, ya, yb, ends, pm, res, mask, sems):
    lane = lane_ids((8, NZ))
    last_x, last_y = NX - 1, NY - 1
    first_x, first_y = last_x * (1 - place[6]), last_y * (1 - place[7])
    pick_y = chooser(place, 1)
    spaced = res.reshape(COMP * RHS, PITCH, NZ)
    spans = [pl.ds(RHS * c, RHS) for c in range(COMP)]
    copies = fetch(
        [(perm_hbm, pm.at[pl.ds(0, COMP)]), (mask_hbm, mask)]
        + [(res_hbm.at[span], spaced.at[span, pl.ds(0, NX * NY)]) for span in spans],
        sems,
    )
    copies[0].wait()
    copies[1].wait()

    for x in range(NX):
        pm[COMP, x] = mask[x].astype(F32)
    for f in range(5):
        acc = jnp.zeros((8, NZ), F32)
        for x in range(NX):
            tile = pm[f, x]
            ya[FACE + f, x : x + 1, :] = pick_y(0, tile[0:1], tile[7:8])
            yb[FACE + f, x : x + 1, :] = pick_y(1, tile[0:1], tile[7:8])
            acc = put_ends(acc, tile, lane, x)
        ends[COMP + f] = acc
    for f in range(5):
        xa[FACE + f] = pm[f, first_x]
        xb[FACE + f] = pm[f, last_x - first_x]

    for c in range(COMP):
        copies[2 + c].wait()
        lines = []
        for x in range(NX):
            acc = jnp.zeros((8, NZ), F32)
            for y in range(NY):
                tile = res[pl.ds(c * RHS * PITCH + x * 8 + y, 8, stride=PITCH), :]
                v0[c, x, y] = tile
                acc = put_ends(acc, tile, lane, x * 8 + y)
            lines.append(acc)
        ends[c] = join(lines, lane)
        for i in range(8):
            xa[c * 8 + i] = v0[c, first_x, i]
            xb[c * 8 + i] = v0[c, last_x - first_x, i]
            ya[c * 8 + i] = v0[c, i, first_y]
            yb[c * 8 + i] = v0[c, i, last_y - first_y]


def face(own, other, masks):
    return (-0.5 / SCALE) * (own + other) * masks


def prepare_kernel(table, pm, sol_hbm, store_hbm, label_hbm, sol, tx, ty, tz, diag, rate, label, sems):
    lane = lane_ids((8, NZ))
    sub = lax.broadcasted_iota(jnp.int32, (8, NZ), 0)
    copies = fetch([(store_hbm, diag), (label_hbm, label), (sol_hbm, sol)], sems)
    copies[0].wait()
    copies[1].wait()

    for x in range(NX):
        m = pm[COMP, x]
        kind = label[x]
        rates = []
        for q in range(6):
            value = jnp.where(kind == 0, table[0, q], jnp.where(kind == 1, table[1, q], table[2, q]))
            rates.append((1.0 / SCALE) * m * value)
            rate[q, x] = rates[q]
        below, above = max(x - 1, 0), min(x + 1, NX - 1)
        m_lo = m * pm[COMP, below] if x else jnp.zeros_like(m)
        m_hi = m * pm[COMP, above] if x < NX - 1 else jnp.zeros_like(m)

        def around(own):
            return [pltpu.roll(own, 1, 0), pltpu.roll(own, 7, 0), pltpu.roll(own, 1, 1), pltpu.roll(own, 127, 1)]

        outer = [sub == 0, sub == 7, lane == 0, lane == 127]
        masks = [jnp.where(edge, 0.0, m * n) for edge, n in zip(outer, around(m))]
        for c in range(COMP):
            own = pm[c, x]
            total = diag[c, x] * (1.0 / SCALE)
            for b in range(COMP):
                if b != c:
                    total = total + rates[pair_index(c, b)]
            tx[c, x] = x_lo = face(own, pm[c, below], m_lo)
            tx[COMP + c, x] = x_hi = face(own, pm[c, above], m_hi)
            sides = [face(own, n, mm) for n, mm in zip(around(own), masks)]
            ty[c, x], ty[COMP + c, x], tz[c, x], tz[COMP + c, x] = sides
            diag[c, x] = total - x_lo - x_hi - sides[0] - sides[1] - sides[2] - sides[3]
    copies[2].wait()


def local_kernel(index, cur, tx, ty, tz, diag, rate, out):
    shift = SHIFTS[index] / SCALE

    def loop(x, _):
        below, above = jnp.maximum(x - 1, 0), jnp.minimum(x + 1, NX - 1)
        low = None
        own = [cur[c, x, 0] for c in range(COMP)]
        for y in range(NY):
            row = pl.ds(y, 1)
            high = [cur[c, x, y + 1] for c in range(COMP)] if y < NY - 1 else None
            rates = [rate[q, x, row, :] for q in range(6)]
            for c in range(COMP):
                p = own[c]
                value = (diag[c, x, row, :] - shift) * p
                side = tx[c, x, row, :] * cur[c, below, y] + tx[COMP + c, x, row, :] * cur[c, above, y]
                if y:
                    value = value + ty[c, x, row, :] * low[c]
                if y < NY - 1:
                    side = side + ty[COMP + c, x, row, :] * high[c]
                value = value + tz[c, x, row, :] * pltpu.roll(p, 1, 1)
                side = side + tz[COMP + c, x, row, :] * pltpu.roll(p, 127, 1)
                others = [b for b in range(COMP) if b != c]
                flow = rates[pair_index(c, others[0])] * own[others[0]]
                for b in others[1:]:
                    flow = flow + rates[pair_index(c, b)] * own[b]
                out[c, x, y] = (value + side) - flow
            low, own = own, high
        return 0

    lax.fori_loop(0, NX, loop, 0)


def ghost_tile(place, first, second, lane):
    return jnp.where(((lane + place[8]) & 1) == 0, second, first)


def edge_kernel(place, inner, halo, bx, by, bz):
    xa, xb, ya, yb, z0, z1 = halo
    pick_x, pick_y = chooser(place, 0), chooser(place, 1)
    lane = lane_ids((8, NZ))
    keep = [place[i].astype(F32) for i in range(6)]
    tiles = [ghost_tile(place, z0[COMP + f], z1[COMP + f], lane) for f in range(5)]
    tiles[4] = tiles[4] * jnp.where((lane & 1) == 0, keep[4], keep[5])
    for side in range(2):
        x = side * (NX - 1)
        near_x = [pick_x(side, xa[FACE + f], xb[FACE + f]) for f in range(5)]
        mask = inner[COMP, x] * near_x[COMP] * keep[side]
        for c in range(COMP):
            bx[side, c] = face(inner[c, x], near_x[c], mask)

    for x in range(NX):
        row = pl.ds(x, 1)
        for side in range(2):
            own = pl.ds(side * (NY - 1), 1)
            near_y = [pick_y(side, ya[FACE + f, row, :], yb[FACE + f, row, :]) for f in range(5)]
            mask = inner[COMP, x, own, :] * near_y[COMP] * keep[2 + side]
            for c in range(COMP):
                by[side, c, row, :] = face(inner[c, x, own, :], near_y[c], mask)
        near_x = [pltpu.roll(t, (128 - 2 * x) & 127, 1) for t in tiles]
        ghosts = [jnp.where(lane == 0, t, pltpu.roll(t, 126, 1)) for t in near_x]
        mask = jnp.where((lane == 0) | (lane == 127), inner[COMP, x] * ghosts[4], 0.0)
        for c in range(COMP):
            bz[c, x] = face(inner[c, x], ghosts[c], mask)


def close_step(place, part, cur, halo, bx, by, bz, out, sends):
    xa, xb, ya, yb, z0, z1 = halo
    pick_x, pick_y = chooser(place, 0), chooser(place, 1)
    lane = lane_ids((8, NZ))
    ghosts, lines = [], [[] for _ in range(COMP)]
    for c in range(COMP):
        tile = ghost_tile(place, z0[c], z1[c], lane)
        ghosts.append(jnp.where((lane & 1) == 0, pltpu.roll(tile, 127, 1), pltpu.roll(tile, 1, 1)))
    for x in range(NX):
        accs = [jnp.zeros((8, NZ), F32) for _ in range(COMP)]
        for y in range(NY):
            slot = x * 8 + y
            for c in range(COMP):
                p = cur[c, x, y]
                g = pltpu.roll(ghosts[c], (127 - 2 * slot) & 127, 1)
                value = part[c, x, y] + bz[c, x, pl.ds(y, 1), :] * (g - p)
                if y in (0, NY - 1):
                    side = 1 if y else 0
                    other = pick_y(side, ya[c * 8 + x], yb[c * 8 + x])
                    value = value + by[side, c, pl.ds(x, 1), :] * (other - p)
                if x in (0, NX - 1):
                    side = 1 if x else 0
                    other = pick_x(side, xa[c * 8 + y], xb[c * 8 + y])
                    value = value + bx[side, c, pl.ds(y, 1), :] * (other - p)
                out[c, x, y] = value
                if sends is not None:
                    accs[c] = put_ends(accs[c], value, lane, slot)
        for c in range(COMP):
            lines[c].append(accs[c])
    if sends is not None:
        for c in range(COMP):
            sends[4][c] = join(lines[c], lane)
        last_x, last_y = NX - 1, NY - 1
        first_x, first_y = last_x * (1 - place[6]), last_y * (1 - place[7])
        for c in range(COMP):
            for i in range(8):
                sends[0][c * 8 + i] = out[c, first_x, i]
                sends[1][c * 8 + i] = out[c, last_x - first_x, i]
                sends[2][c * 8 + i] = out[c, i, first_y]
                sends[3][c * 8 + i] = out[c, i, last_y - first_y]


def first_kernel(place, part, cur, inner, *refs):
    halo, refs = refs[:6], refs[6:]
    out, sends, faces = refs[0], refs[1:6], refs[6:9]
    edge_kernel(place, inner, halo, *faces)
    close_step(place, part, cur, halo, *faces, out, sends)


def step_kernel(place, piece, part, cur, *refs):
    halo, faces, refs = refs[:6], refs[6:9], refs[9:]
    out, sends = refs[0], refs[1:] or None
    close_step(place, part, cur, halo, *faces, out, sends)


def gram_kernel(index, cur, *refs):
    others = [a for a, b in BLOCKS if b == index]
    count = len(others)
    older, refs = refs[: count - (index < S)], refs[count - (index < S) :]
    before = None
    if index:
        before, refs = refs[0], refs[1:]
    split, out = refs
    lane = lane_ids((8, NZ))
    tall = 16 * count

    def loop(x, total):
        tiles = []
        for c in range(COMP):
            for y in range(NY):
                v = cur[c, x, y]
                high = v.astype(BF16).astype(F32)
                tile = jnp.concatenate([high, v - high], 0).astype(BF16)
                split[c, x, y] = tile
                tiles.append(tile)
        right = jnp.concatenate(tiles, 1)
        lefts = [
            jnp.concatenate([old[c, x, y] for c in range(COMP) for y in range(NY)], 1) for old in older
        ]
        if index < S:
            lefts.append(right)
        left = jnp.concatenate(lefts, 0) if len(lefts) > 1 else lefts[0]
        return total + lax.dot_general(
            left, right, (((1,), (1,)), ((), ())), preferred_element_type=F32
        )

    total = lax.fori_loop(0, NX, loop, jnp.zeros((tall, 16), F32))
    wide = jnp.concatenate([total, jnp.zeros((tall, NZ - 16), F32)], 1)
    value = jnp.zeros((8, NZ), F32)
    for number, a in enumerate(others):
        top = 16 * number
        both = wide[top : top + 8] + wide[top + 8 : top + 16]
        both = both + pltpu.roll(both, NZ - 8, 1)
        slot = BLOCKS.index((a, index))
        value = jnp.where((lane >> 3) == slot, pltpu.roll(both, 8 * slot, 1), value)
    if index:
        value = value + before[...]
    if index < S:
        out[...] = value
    else:
        for copy in range(out.shape[0]):
            out[copy] = value


def relay_kernel(parts, out):
    total = parts[0]
    for i in range(1, parts.shape[0]):
        total = total + parts[i]
    for copy in range(out.shape[0]):
        out[copy] = total


def lane_group(tile, source, target):
    return pltpu.roll(tile, (8 * (target - source)) % NZ, 1)


def factor(packed, weight):
    lane8 = lane_ids((8, NZ)) >> 3
    turned = jnp.transpose(jnp.concatenate([packed, jnp.zeros((NZ - 8, NZ), F32)], 0))
    rows = []
    for a in range(S):
        line = jnp.zeros((8, NZ), F32)
        for b in range(S + 1):
            if b == S and a < S - 1:
                block = lane_group(packed, BLOCKS.index((a + 1, 3)), b)
                block = block + (SHIFTS[a] - SHIFTS[3]) / SCALE * lane_group(
                    packed, BLOCKS.index((a, 3)), b
                )
            elif a <= b:
                block = lane_group(packed, BLOCKS.index((a, b)), b)
            else:
                slot = BLOCKS.index((b, a))
                block = lane_group(turned[8 * slot : 8 * slot + 8], 0, b)
            if a == b:
                slot = BLOCKS.index((a, a))
                other = lane_group(turned[8 * slot : 8 * slot + 8], 0, b)
                block = 0.5 * (block + other)
            line = jnp.where(lane8 == b, block, line)
        rows.append(line)
    gram = jnp.concatenate(rows, 0)
    lane = lane_ids((32, NZ))
    row = lax.broadcasted_iota(jnp.int32, (32, NZ), 0)
    group = lane >> 3
    sigma = jnp.where(
        group == 0, SHIFTS[0], jnp.where(group == 1, SHIFTS[1], jnp.where(group == 2, SHIFTS[2], SHIFTS[3]))
    )
    moment = jnp.where(lane < 32, sigma * gram + SCALE * pltpu.roll(gram, NZ - 8, 1), 0.0)
    flipped = jnp.transpose(jnp.concatenate([moment, jnp.zeros((NZ - 32, NZ), F32)], 0))[:32]
    moment = 0.5 * (moment + flipped)
    left = jnp.where(lane < 32, gram, jnp.where(lane == row + 32, 1.0, 0.0))
    right = jnp.where(lane < 32, moment, jnp.where(group == 4, pltpu.roll(gram, 32, 1), 0.0))
    inverse = jnp.zeros((32, NZ), F32)
    for j in range(0, 32, 2):
        kept = []
        for matrix in (left, right):
            c0 = jnp.broadcast_to(matrix[:, j : j + 1], (32, NZ))
            c1 = jnp.broadcast_to(matrix[:, j + 1 : j + 2], (32, NZ))
            r0, r1 = matrix[j : j + 1], matrix[j + 1 : j + 2]
            p, q, r = c0[j : j + 1], c1[j : j + 1], c1[j + 1 : j + 2]
            inv = 1.0 / (p * r - q * q)
            n0, n1 = (r * r0 - q * r1) * inv, (p * r1 - q * r0) * inv
            kept.append((matrix - c0 * n0 - c1 * n1, r0, r1, p, q, r, n0, n1))
        left, r0, r1, p, q, r, _, _ = kept[0]
        ratio = q / p
        inverse = jnp.where(row == j, r0 * lax.rsqrt(p), inverse)
        inverse = jnp.where(row == j + 1, (r1 - ratio * r0) * lax.rsqrt(r - q * ratio), inverse)
        right, n0, n1 = kept[1][0], kept[1][6], kept[1][7]
        right = jnp.where(row == j, n0, jnp.where(row == j + 1, n1, right))
    inverse = pltpu.roll(inverse, NZ - 32, 1)
    coeff = pltpu.roll(right, NZ - 32, 1)
    coeff = jnp.transpose(jnp.concatenate([coeff, jnp.zeros((NZ - 32, NZ), F32)], 0))[:8]
    coeff = jnp.where(lane8 < S, coeff, 0.0)
    ext = SCALE * pltpu.roll(coeff, 8, 1)
    for k in range(S):
        ext = jnp.where(lane8 == k, ext + SHIFTS[k] * coeff, ext)
    full = jnp.concatenate([jnp.where(lane < 32, inverse, 0.0), coeff, ext], 0)
    lanes = lane_ids((48, NZ))
    spread = jnp.zeros((48, NZ), F32)
    for k in range(S + 1):
        for part in range(2):
            spread = jnp.where(
                (lanes >> 3) == 2 * k + part, pltpu.roll(full, (8 * (2 * k + part - k)) % NZ, 1), spread
            )
    high = spread.astype(BF16)
    low = (spread - high.astype(F32)).astype(BF16)
    weight[0:48] = high
    weight[48:96] = low


def finish_kernel(packed, s0, s1, s2, s3, s4, sol, v0, sol_hbm, res_hbm, basis_hbm, new_sol, new_res, basis, weight, sems):
    total = packed[0]
    for i in range(1, packed.shape[0]):
        total = total + packed[i]
    factor(total, weight)
    copies = []
    for c in range(COMP):
        for half in range(2):
            spots = [(4 * half + u, y) for u in range(4) for y in range(NY)]
            lines = [jnp.concatenate([s[c, x, y] for x, y in spots], 1) for s in (s0, s1, s2, s3, s4)]
            both = jnp.dot(weight[:, 0:80], jnp.concatenate(lines, 0), preferred_element_type=F32)
            both = both[0:48] + both[48:96]
            for number, (x, y) in enumerate(spots):
                place = x * 8 + y
                part = both[:, number * NZ : (number + 1) * NZ]
                for q in range(0, S * RHS, 8):
                    first = (c * S * RHS + q) * PITCH + place
                    basis[pl.ds(first, 8, stride=PITCH), :] = part[q : q + 8]
                spot = pl.ds(c * RHS * PITCH + place, 8, stride=PITCH)
                old = sol[pl.ds(c * RHS * NX * NY + place, 8, stride=NX * NY), :]
                new_sol[spot, :] = old + part[32:40]
                new_res[spot, :] = v0[c, x, y] - part[40:48]
        pieces = ((basis, basis_hbm, S * RHS), (new_sol, sol_hbm, RHS), (new_res, res_hbm, RHS))
        for number, (source, target, count) in enumerate(pieces):
            spaced = source.reshape(source.shape[0] // PITCH, PITCH, NZ)
            span = pl.ds(c * count, count)
            copies.append(
                pltpu.make_async_copy(
                    spaced.at[span, pl.ds(0, NX * NY)], target.at[span], sems.at[c, number]
                )
            )
            copies[-1].start()
    for copy in copies:
        copy.wait()


def shaped(*shape, dtype=F32):
    return jax.ShapeDtypeStruct(shape, dtype)


def near(*shape, dtype=F32):
    return pltpu.VMEM(shape, dtype)


def far(array):
    return pltpu.with_memory_space_constraint(array, pltpu.HBM)


def params(mib):
    return pltpu.CompilerParams(vmem_limit_bytes=mib << 20)


def exchange(sends):
    moved = []
    for axis, pair in (("gx", sends[0:2]), ("gy", sends[2:4]), ("gz", (sends[4], sends[4]))):
        count = lax.axis_size(axis)
        first = [(i, i ^ 1) for i in range(count)]
        second = [(i, (i + (1 if i % 2 else -1)) % count) for i in range(count)]
        moved.append(lax.ppermute(pair[0], axis, first))
        moved.append(lax.ppermute(pair[1], axis, second))
    return moved


def body(solution, residual, permeability, storage, tissue_mask, tissue_label, exchange_table):
    flat = residual.reshape(COMP * RHS, NX * NY, NZ)
    edge = []
    for axis in ("gx", "gy", "gz"):
        place = lax.axis_index(axis)
        edge += [place > 0, place < lax.axis_size(axis) - 1]
    edge += [lax.axis_index(axis) % 2 == 1 for axis in ("gx", "gy", "gz")]
    edge = jnp.stack(edge).astype(jnp.int32)
    field = near(COMP, NX, NY, RHS, NZ)
    face = near(FACE + 5, 8, NZ)
    total = COMP * RHS * NX * NY
    in_hbm = pl.BlockSpec(memory_space=pltpu.HBM)
    v0, *sends, inner = pl.pallas_call(
        pack_kernel,
        out_shape=(field, face, face, face, face, face, near(5, NX, NY, NZ)),
        in_specs=[SMEM] + [in_hbm] * 3,
        out_specs=[VMEM] * 7,
        scratch_shapes=[
            pltpu.VMEM((COMP * RHS * PITCH, NZ), F32),
            pltpu.VMEM((NX, NY, NZ), jnp.int32),
            pltpu.SemaphoreType.DMA((2 + COMP,)),
        ],
        compiler_params=params(5),
        name="pack",
    )(edge, far(flat), far(permeability), far(tissue_mask))

    wide, tall = lax.axis_size("gx") * lax.axis_size("gz"), lax.axis_size("gy")

    def gram(index, current, older, before):
        inputs = [current, *(older if index < S else older[-1:]), *before]
        return pl.pallas_call(
            lambda *refs: gram_kernel(index, *refs),
            out_shape=(
                near(COMP, NX, NY, 16, NZ, dtype=BF16),
                near(8, NZ) if index < S else near(wide, 8, NZ),
            ),
            in_specs=[VMEM] * len(inputs),
            out_specs=[VMEM] * 2,
            compiler_params=params(5),
            cost_estimate=pl.CostEstimate(
                flops=2 * 16 * 16 * (index + 1) * 32768, bytes_accessed=(3 + index) << 20, transcendentals=0
            ),
            name=f"gram{index}",
        )(*inputs)

    halo = exchange(sends)
    splits = []
    plane = near(COMP, NX, NY, NZ)
    double = near(2 * COMP, NX, NY, NZ)
    sol, *coef = pl.pallas_call(
        prepare_kernel,
        out_shape=(near(total, NZ), double, double, double, plane, near(6, NX, NY, NZ)),
        in_specs=[SMEM, VMEM] + [in_hbm] * 3,
        out_specs=[VMEM] * 6,
        scratch_shapes=[pltpu.VMEM((NX, NY, NZ), jnp.int32), pltpu.SemaphoreType.DMA((3,))],
        compiler_params=params(5),
        name="prepare",
    )(exchange_table, inner, far(solution.reshape(total, NZ)), far(storage), far(tissue_label))

    def local(index, current):
        return pl.pallas_call(
            lambda *refs: local_kernel(index, *refs),
            out_shape=field,
            in_specs=[VMEM] * 6,
            out_specs=VMEM,
            compiler_params=params(5),
            cost_estimate=pl.CostEstimate(flops=6 << 20, bytes_accessed=3 << 20, transcendentals=0),
            name=f"local{index + 1}",
        )(current, *coef)

    part = local(0, v0)
    split, piece = gram(0, v0, [], [])
    splits.append(split)
    face = near(FACE, 8, NZ)
    results = pl.pallas_call(
        first_kernel,
        out_shape=[field] + [face] * 5 + [near(2, COMP, NY, NZ), near(2, COMP, NX, NZ), plane],
        in_specs=[SMEM] + [VMEM] * 9,
        out_specs=[VMEM] * 9,
        compiler_params=params(5),
        name="step1",
    )(edge, part, v0, inner, *halo)
    current, sends, faces = results[0], results[1:6], results[6:]
    for index in range(1, S):
        halo = exchange(sends)
        part = local(index, current)
        split, piece = gram(index, current, splits, [piece])
        splits.append(split)
        outs = [field] + ([face] * 5 if index < S - 1 else [])
        results = pl.pallas_call(
            step_kernel,
            out_shape=outs,
            in_specs=[SMEM] + [VMEM] * 12,
            out_specs=[VMEM] * len(outs),
                compiler_params=params(5),
            name=f"step{index + 1}",
        )(edge, piece, part, current, *halo, *faces)
        current, sends = results[0], results[1:]
    split, piece = gram(S, current, splits, [piece])
    splits.append(split)
    parts = lax.all_to_all(piece, ("gx", "gz"), 0, 0)
    parts = pl.pallas_call(
        relay_kernel,
        out_shape=near(tall, 8, NZ),
        in_specs=[VMEM],
        out_specs=VMEM,
        compiler_params=params(2),
        name="relay",
    )(parts)
    packed = lax.all_to_all(parts, ("gy",), 0, 0)
    count = COMP * RHS
    new_sol, new_res, basis = pl.pallas_call(
        finish_kernel,
        out_shape=(shaped(count, NX * NY, NZ), shaped(count, NX * NY, NZ), shaped(S * count, NX * NY, NZ)),
        in_specs=[VMEM] * 8,
        out_specs=[in_hbm] * 3,
        scratch_shapes=[
            pltpu.VMEM((count * PITCH, NZ), F32),
            pltpu.VMEM((count * PITCH, NZ), F32),
            pltpu.VMEM((S * count * PITCH, NZ), F32),
            pltpu.VMEM((96, NZ), BF16),
            pltpu.SemaphoreType.DMA((COMP, 3)),
        ],
        compiler_params=params(24),
        name="finish",
    )(packed, *splits, sol, v0)
    return (
        new_sol.reshape(solution.shape),
        new_res.reshape(residual.shape),
        basis.reshape((COMP, S * RHS) + solution.shape[2:]),
    )


def solution(mesh):
    wide = P(None, None, "gx", "gy", "gz")
    return jax.shard_map(
        body,
        mesh=mesh,
        in_specs=(
            wide,
            wide,
            P(None, "gx", "gy", "gz"),
            P(None, "gx", "gy", "gz"),
            P("gx", "gy", "gz"),
            P("gx", "gy", "gz"),
            P(),
        ),
        out_specs=(wide, wide, wide),
        check_vma=False,
    )
```

```python
import jax
import jax.numpy as jnp
from jax import lax
from jax.experimental import pallas as pl
from jax.experimental.pallas import tpu as pltpu
from jax.sharding import PartitionSpec as P

COMP = 4
RHS = 8
S = 4
PAIRS = ((0, 1), (0, 2), (0, 3), (1, 2), (1, 3), (2, 3))
SHIFTS = (2.0, 14.0, 6.0, 10.0)
SCALE = 8.0
F32 = jnp.float32
BF16 = jnp.bfloat16

PITCH = 72
NX, NY, NZ = 8, 8, 128
FACE = COMP * 8
BLOCKS = tuple((a, b) for b in range(4) for a in range(b + 1)) + ((3, 4),)
VMEM = pl.BlockSpec(memory_space=pltpu.VMEM)
SMEM = pl.BlockSpec(memory_space=pltpu.SMEM)


def pair_index(a, b):
    return PAIRS.index((min(a, b), max(a, b)))


def lane_ids(shape):
    return lax.broadcasted_iota(jnp.int32, shape, len(shape) - 1)


def put_ends(acc, tile, lane, slot):
    return jnp.where((lane >> 1) == slot, pltpu.roll(tile, 2 * slot + 1, 1), acc)


def chooser(place, axis):
    odd = (jnp.zeros((8, NZ), jnp.int32) + place[6 + axis]) == 1

    def pick(side, first, second):
        mask = odd[: first.shape[0]]
        return jnp.where(mask, second, first) if side else jnp.where(mask, first, second)

    return pick


def join(lines, lane):
    while len(lines) > 1:
        half = 128 // len(lines)
        lines = [
            jnp.where((lane & half) == 0, low, high) for low, high in zip(lines[::2], lines[1::2])
        ]
    return lines[0]


def fetch(pairs, sems):
    copies = [pltpu.make_async_copy(src, dst, sems.at[i]) for i, (src, dst) in enumerate(pairs)]
    for copy in copies:
        copy.start()
    return copies


def pack_kernel(place, res_hbm, perm_hbm, mask_hbm, v0, xa, xb, ya, yb, ends, pm, res, mask, sems):
    lane = lane_ids((8, NZ))
    last_x, last_y = NX - 1, NY - 1
    first_x, first_y = last_x * (1 - place[6]), last_y * (1 - place[7])
    pick_y = chooser(place, 1)
    spaced = res.reshape(COMP * RHS, PITCH, NZ)
    spans = [pl.ds(RHS * c, RHS) for c in range(COMP)]
    copies = fetch(
        [(perm_hbm, pm.at[pl.ds(0, COMP)]), (mask_hbm, mask)]
        + [(res_hbm.at[span], spaced.at[span, pl.ds(0, NX * NY)]) for span in spans],
        sems,
    )
    copies[0].wait()
    copies[1].wait()

    for x in range(NX):
        pm[COMP, x] = mask[x].astype(F32)
    for f in range(5):
        acc = jnp.zeros((8, NZ), F32)
        for x in range(NX):
            tile = pm[f, x]
            ya[FACE + f, x : x + 1, :] = pick_y(0, tile[0:1], tile[7:8])
            yb[FACE + f, x : x + 1, :] = pick_y(1, tile[0:1], tile[7:8])
            acc = put_ends(acc, tile, lane, x)
        ends[COMP + f] = acc
    for f in range(5):
        xa[FACE + f] = pm[f, first_x]
        xb[FACE + f] = pm[f, last_x - first_x]

    for c in range(COMP):
        copies[2 + c].wait()
        lines = []
        for x in range(NX):
            acc = jnp.zeros((8, NZ), F32)
            for y in range(NY):
                tile = res[pl.ds(c * RHS * PITCH + x * 8 + y, 8, stride=PITCH), :]
                v0[c, x, y] = tile
                acc = put_ends(acc, tile, lane, x * 8 + y)
            lines.append(acc)
        ends[c] = join(lines, lane)
        for i in range(8):
            xa[c * 8 + i] = v0[c, first_x, i]
            xb[c * 8 + i] = v0[c, last_x - first_x, i]
            ya[c * 8 + i] = v0[c, i, first_y]
            yb[c * 8 + i] = v0[c, i, last_y - first_y]


def face(own, other, masks):
    return (-0.5 / SCALE) * (own + other) * masks


def prepare_kernel(table, pm, sol_hbm, store_hbm, label_hbm, sol, tx, ty, tz, diag, rate, label, sems):
    lane = lane_ids((8, NZ))
    sub = lax.broadcasted_iota(jnp.int32, (8, NZ), 0)
    copies = fetch([(store_hbm, diag), (label_hbm, label), (sol_hbm, sol)], sems)
    copies[0].wait()
    copies[1].wait()

    for x in range(NX):
        m = pm[COMP, x]
        kind = label[x]
        rates = []
        for q in range(6):
            value = jnp.where(kind == 0, table[0, q], jnp.where(kind == 1, table[1, q], table[2, q]))
            rates.append((1.0 / SCALE) * m * value)
            rate[q, x] = rates[q]
        below, above = max(x - 1, 0), min(x + 1, NX - 1)
        m_lo = m * pm[COMP, below] if x else jnp.zeros_like(m)
        m_hi = m * pm[COMP, above] if x < NX - 1 else jnp.zeros_like(m)

        def around(own):
            return [pltpu.roll(own, 1, 0), pltpu.roll(own, 7, 0), pltpu.roll(own, 1, 1), pltpu.roll(own, 127, 1)]

        outer = [sub == 0, sub == 7, lane == 0, lane == 127]
        masks = [jnp.where(edge, 0.0, m * n) for edge, n in zip(outer, around(m))]
        for c in range(COMP):
            own = pm[c, x]
            total = diag[c, x] * (1.0 / SCALE)
            for b in range(COMP):
                if b != c:
                    total = total + rates[pair_index(c, b)]
            tx[c, x] = x_lo = face(own, pm[c, below], m_lo)
            tx[COMP + c, x] = x_hi = face(own, pm[c, above], m_hi)
            sides = [face(own, n, mm) for n, mm in zip(around(own), masks)]
            ty[c, x], ty[COMP + c, x], tz[c, x], tz[COMP + c, x] = sides
            diag[c, x] = total - x_lo - x_hi - sides[0] - sides[1] - sides[2] - sides[3]
    copies[2].wait()


def local_kernel(index, cur, tx, ty, tz, diag, rate, out):
    shift = SHIFTS[index] / SCALE

    def loop(x, _):
        below, above = jnp.maximum(x - 1, 0), jnp.minimum(x + 1, NX - 1)
        low = None
        own = [cur[c, x, 0] for c in range(COMP)]
        for y in range(NY):
            row = pl.ds(y, 1)
            high = [cur[c, x, y + 1] for c in range(COMP)] if y < NY - 1 else None
            rates = [rate[q, x, row, :] for q in range(6)]
            for c in range(COMP):
                p = own[c]
                value = (diag[c, x, row, :] - shift) * p
                side = tx[c, x, row, :] * cur[c, below, y] + tx[COMP + c, x, row, :] * cur[c, above, y]
                if y:
                    value = value + ty[c, x, row, :] * low[c]
                if y < NY - 1:
                    side = side + ty[COMP + c, x, row, :] * high[c]
                value = value + tz[c, x, row, :] * pltpu.roll(p, 1, 1)
                side = side + tz[COMP + c, x, row, :] * pltpu.roll(p, 127, 1)
                others = [b for b in range(COMP) if b != c]
                flow = rates[pair_index(c, others[0])] * own[others[0]]
                for b in others[1:]:
                    flow = flow + rates[pair_index(c, b)] * own[b]
                out[c, x, y] = (value + side) - flow
            low, own = own, high
        return 0

    lax.fori_loop(0, NX, loop, 0)


def ghost_tile(place, first, second, lane):
    return jnp.where(((lane + place[8]) & 1) == 0, second, first)


def edge_kernel(place, inner, halo, bx, by, bz):
    xa, xb, ya, yb, z0, z1 = halo
    pick_x, pick_y = chooser(place, 0), chooser(place, 1)
    lane = lane_ids((8, NZ))
    keep = [place[i].astype(F32) for i in range(6)]
    tiles = [ghost_tile(place, z0[COMP + f], z1[COMP + f], lane) for f in range(5)]
    tiles[4] = tiles[4] * jnp.where((lane & 1) == 0, keep[4], keep[5])
    for side in range(2):
        x = side * (NX - 1)
        near_x = [pick_x(side, xa[FACE + f], xb[FACE + f]) for f in range(5)]
        mask = inner[COMP, x] * near_x[COMP] * keep[side]
        for c in range(COMP):
            bx[side, c] = face(inner[c, x], near_x[c], mask)

    for x in range(NX):
        row = pl.ds(x, 1)
        for side in range(2):
            own = pl.ds(side * (NY - 1), 1)
            near_y = [pick_y(side, ya[FACE + f, row, :], yb[FACE + f, row, :]) for f in range(5)]
            mask = inner[COMP, x, own, :] * near_y[COMP] * keep[2 + side]
            for c in range(COMP):
                by[side, c, row, :] = face(inner[c, x, own, :], near_y[c], mask)
        near_x = [pltpu.roll(t, (128 - 2 * x) & 127, 1) for t in tiles]
        ghosts = [jnp.where(lane == 0, t, pltpu.roll(t, 126, 1)) for t in near_x]
        mask = jnp.where((lane == 0) | (lane == 127), inner[COMP, x] * ghosts[4], 0.0)
        for c in range(COMP):
            bz[c, x] = face(inner[c, x], ghosts[c], mask)


def close_step(place, part, cur, halo, bx, by, bz, out, sends):
    xa, xb, ya, yb, z0, z1 = halo
    pick_x, pick_y = chooser(place, 0), chooser(place, 1)
    lane = lane_ids((8, NZ))
    ghosts, lines = [], [[] for _ in range(COMP)]
    for c in range(COMP):
        tile = ghost_tile(place, z0[c], z1[c], lane)
        ghosts.append(jnp.where((lane & 1) == 0, pltpu.roll(tile, 127, 1), pltpu.roll(tile, 1, 1)))
    for x in range(NX):
        accs = [jnp.zeros((8, NZ), F32) for _ in range(COMP)]
        for y in range(NY):
            slot = x * 8 + y
            for c in range(COMP):
                p = cur[c, x, y]
                g = pltpu.roll(ghosts[c], (127 - 2 * slot) & 127, 1)
                value = part[c, x, y] + bz[c, x, pl.ds(y, 1), :] * (g - p)
                if y in (0, NY - 1):
                    side = 1 if y else 0
                    other = pick_y(side, ya[c * 8 + x], yb[c * 8 + x])
                    value = value + by[side, c, pl.ds(x, 1), :] * (other - p)
                if x in (0, NX - 1):
                    side = 1 if x else 0
                    other = pick_x(side, xa[c * 8 + y], xb[c * 8 + y])
                    value = value + bx[side, c, pl.ds(y, 1), :] * (other - p)
                out[c, x, y] = value
                if sends is not None:
                    accs[c] = put_ends(accs[c], value, lane, slot)
        for c in range(COMP):
            lines[c].append(accs[c])
    if sends is not None:
        for c in range(COMP):
            sends[4][c] = join(lines[c], lane)
        last_x, last_y = NX - 1, NY - 1
        first_x, first_y = last_x * (1 - place[6]), last_y * (1 - place[7])
        for c in range(COMP):
            for i in range(8):
                sends[0][c * 8 + i] = out[c, first_x, i]
                sends[1][c * 8 + i] = out[c, last_x - first_x, i]
                sends[2][c * 8 + i] = out[c, i, first_y]
                sends[3][c * 8 + i] = out[c, i, last_y - first_y]


def first_kernel(place, part, cur, inner, *refs):
    halo, refs = refs[:6], refs[6:]
    out, sends, faces = refs[0], refs[1:6], refs[6:9]
    edge_kernel(place, inner, halo, *faces)
    close_step(place, part, cur, halo, *faces, out, sends)


def step_kernel(place, piece, part, cur, *refs):
    halo, faces, refs = refs[:6], refs[6:9], refs[9:]
    out, sends = refs[0], refs[1:] or None
    close_step(place, part, cur, halo, *faces, out, sends)


def gram_kernel(index, cur, *refs):
    others = [a for a, b in BLOCKS if b == index]
    count = len(others)
    older, refs = refs[: count - (index < S)], refs[count - (index < S) :]
    before = None
    if index:
        before, refs = refs[0], refs[1:]
    split, out = refs
    lane = lane_ids((8, NZ))
    tall = 16 * count

    def loop(x, total):
        tiles = []
        for c in range(COMP):
            for y in range(NY):
                v = cur[c, x, y]
                high = v.astype(BF16).astype(F32)
                tile = jnp.concatenate([high, v - high], 0).astype(BF16)
                split[c, x, y] = tile
                tiles.append(tile)
        right = jnp.concatenate(tiles, 1)
        lefts = [
            jnp.concatenate([old[c, x, y] for c in range(COMP) for y in range(NY)], 1) for old in older
        ]
        if index < S:
            lefts.append(right)
        left = jnp.concatenate(lefts, 0) if len(lefts) > 1 else lefts[0]
        return total + lax.dot_general(
            left, right, (((1,), (1,)), ((), ())), preferred_element_type=F32
        )

    total = lax.fori_loop(0, NX, loop, jnp.zeros((tall, 16), F32))
    wide = jnp.concatenate([total, jnp.zeros((tall, NZ - 16), F32)], 1)
    value = jnp.zeros((8, NZ), F32)
    for number, a in enumerate(others):
        top = 16 * number
        both = wide[top : top + 8] + wide[top + 8 : top + 16]
        both = both + pltpu.roll(both, NZ - 8, 1)
        slot = BLOCKS.index((a, index))
        value = jnp.where((lane >> 3) == slot, pltpu.roll(both, 8 * slot, 1), value)
    if index:
        value = value + before[...]
    if index < S:
        out[...] = value
    else:
        for copy in range(out.shape[0]):
            out[copy] = value


def relay_kernel(parts, out):
    total = parts[0]
    for i in range(1, parts.shape[0]):
        total = total + parts[i]
    for copy in range(out.shape[0]):
        out[copy] = total


def lane_group(tile, source, target):
    return pltpu.roll(tile, (8 * (target - source)) % NZ, 1)


def factor(packed, weight):
    lane8 = lane_ids((8, NZ)) >> 3
    turned = jnp.transpose(jnp.concatenate([packed, jnp.zeros((NZ - 8, NZ), F32)], 0))
    rows = []
    for a in range(S):
        line = jnp.zeros((8, NZ), F32)
        for b in range(S + 1):
            if b == S and a < S - 1:
                block = lane_group(packed, BLOCKS.index((a + 1, 3)), b)
                block = block + (SHIFTS[a] - SHIFTS[3]) / SCALE * lane_group(
                    packed, BLOCKS.index((a, 3)), b
                )
            elif a <= b:
                block = lane_group(packed, BLOCKS.index((a, b)), b)
            else:
                slot = BLOCKS.index((b, a))
                block = lane_group(turned[8 * slot : 8 * slot + 8], 0, b)
            if a == b:
                slot = BLOCKS.index((a, a))
                other = lane_group(turned[8 * slot : 8 * slot + 8], 0, b)
                block = 0.5 * (block + other)
            line = jnp.where(lane8 == b, block, line)
        rows.append(line)
    gram = jnp.concatenate(rows, 0)
    lane = lane_ids((32, NZ))
    row = lax.broadcasted_iota(jnp.int32, (32, NZ), 0)
    group = lane >> 3
    sigma = jnp.where(
        group == 0, SHIFTS[0], jnp.where(group == 1, SHIFTS[1], jnp.where(group == 2, SHIFTS[2], SHIFTS[3]))
    )
    moment = jnp.where(lane < 32, sigma * gram + SCALE * pltpu.roll(gram, NZ - 8, 1), 0.0)
    flipped = jnp.transpose(jnp.concatenate([moment, jnp.zeros((NZ - 32, NZ), F32)], 0))[:32]
    moment = 0.5 * (moment + flipped)
    left = jnp.where(lane < 32, gram, jnp.where(lane == row + 32, 1.0, 0.0))
    right = jnp.where(lane < 32, moment, jnp.where(group == 4, pltpu.roll(gram, 32, 1), 0.0))
    inverse = jnp.zeros((32, NZ), F32)
    for j in range(0, 32, 2):
        kept = []
        for matrix in (left, right):
            c0 = jnp.broadcast_to(matrix[:, j : j + 1], (32, NZ))
            c1 = jnp.broadcast_to(matrix[:, j + 1 : j + 2], (32, NZ))
            r0, r1 = matrix[j : j + 1], matrix[j + 1 : j + 2]
            p, q, r = c0[j : j + 1], c1[j : j + 1], c1[j + 1 : j + 2]
            inv = 1.0 / (p * r - q * q)
            n0, n1 = (r * r0 - q * r1) * inv, (p * r1 - q * r0) * inv
            kept.append((matrix - c0 * n0 - c1 * n1, r0, r1, p, q, r, n0, n1))
        left, r0, r1, p, q, r, _, _ = kept[0]
        ratio = q / p
        inverse = jnp.where(row == j, r0 * lax.rsqrt(p), inverse)
        inverse = jnp.where(row == j + 1, (r1 - ratio * r0) * lax.rsqrt(r - q * ratio), inverse)
        right, n0, n1 = kept[1][0], kept[1][6], kept[1][7]
        right = jnp.where(row == j, n0, jnp.where(row == j + 1, n1, right))
    inverse = pltpu.roll(inverse, NZ - 32, 1)
    coeff = pltpu.roll(right, NZ - 32, 1)
    coeff = jnp.transpose(jnp.concatenate([coeff, jnp.zeros((NZ - 32, NZ), F32)], 0))[:8]
    coeff = jnp.where(lane8 < S, coeff, 0.0)
    ext = SCALE * pltpu.roll(coeff, 8, 1)
    for k in range(S):
        ext = jnp.where(lane8 == k, ext + SHIFTS[k] * coeff, ext)
    full = jnp.concatenate([jnp.where(lane < 32, inverse, 0.0), coeff, ext], 0)
    lanes = lane_ids((48, NZ))
    spread = jnp.zeros((48, NZ), F32)
    for k in range(S + 1):
        for part in range(2):
            spread = jnp.where(
                (lanes >> 3) == 2 * k + part, pltpu.roll(full, (8 * (2 * k + part - k)) % NZ, 1), spread
            )
    high = spread.astype(BF16)
    low = (spread - high.astype(F32)).astype(BF16)
    weight[0:48] = high
    weight[48:96] = low


def finish_kernel(packed, s0, s1, s2, s3, s4, sol, v0, sol_hbm, res_hbm, basis_hbm, new_sol, new_res, basis, weight, sems):
    total = packed[0]
    for i in range(1, packed.shape[0]):
        total = total + packed[i]
    factor(total, weight)
    copies = []
    for c in range(COMP):
        for half in range(2):
            spots = [(4 * half + u, y) for u in range(4) for y in range(NY)]
            lines = [jnp.concatenate([s[c, x, y] for x, y in spots], 1) for s in (s0, s1, s2, s3, s4)]
            both = jnp.dot(weight[:, 0:80], jnp.concatenate(lines, 0), preferred_element_type=F32)
            both = both[0:48] + both[48:96]
            for number, (x, y) in enumerate(spots):
                place = x * 8 + y
                part = both[:, number * NZ : (number + 1) * NZ]
                for q in range(0, S * RHS, 8):
                    first = (c * S * RHS + q) * PITCH + place
                    basis[pl.ds(first, 8, stride=PITCH), :] = part[q : q + 8]
                spot = pl.ds(c * RHS * PITCH + place, 8, stride=PITCH)
                old = sol[pl.ds(c * RHS * NX * NY + place, 8, stride=NX * NY), :]
                new_sol[spot, :] = old + part[32:40]
                new_res[spot, :] = v0[c, x, y] - part[40:48]
        pieces = ((basis, basis_hbm, S * RHS), (new_sol, sol_hbm, RHS), (new_res, res_hbm, RHS))
        for number, (source, target, count) in enumerate(pieces):
            spaced = source.reshape(source.shape[0] // PITCH, PITCH, NZ)
            span = pl.ds(c * count, count)
            copies.append(
                pltpu.make_async_copy(
                    spaced.at[span, pl.ds(0, NX * NY)], target.at[span], sems.at[c, number]
                )
            )
            copies[-1].start()
    for copy in copies:
        copy.wait()


def shaped(*shape, dtype=F32):
    return jax.ShapeDtypeStruct(shape, dtype)


def near(*shape, dtype=F32):
    return pltpu.VMEM(shape, dtype)


def far(array):
    return pltpu.with_memory_space_constraint(array, pltpu.HBM)


def params(mib):
    return pltpu.CompilerParams(vmem_limit_bytes=mib << 20)


def exchange(sends):
    moved = []
    for axis, pair in (("gx", sends[0:2]), ("gy", sends[2:4]), ("gz", (sends[4], sends[4]))):
        count = lax.axis_size(axis)
        first = [(i, i ^ 1) for i in range(count)]
        second = [(i, (i + (1 if i % 2 else -1)) % count) for i in range(count)]
        moved.append(lax.ppermute(pair[0], axis, first))
        moved.append(lax.ppermute(pair[1], axis, second))
    return moved


def body(solution, residual, permeability, storage, tissue_mask, tissue_label, exchange_table):
    flat = residual.reshape(COMP * RHS, NX * NY, NZ)
    edge = []
    for axis in ("gx", "gy", "gz"):
        place = lax.axis_index(axis)
        edge += [place > 0, place < lax.axis_size(axis) - 1]
    edge += [lax.axis_index(axis) % 2 == 1 for axis in ("gx", "gy", "gz")]
    edge = jnp.stack(edge).astype(jnp.int32)
    field = near(COMP, NX, NY, RHS, NZ)
    face = near(FACE + 5, 8, NZ)
    total = COMP * RHS * NX * NY
    in_hbm = pl.BlockSpec(memory_space=pltpu.HBM)
    v0, *sends, inner = pl.pallas_call(
        pack_kernel,
        out_shape=(field, face, face, face, face, face, near(5, NX, NY, NZ)),
        in_specs=[SMEM] + [in_hbm] * 3,
        out_specs=[VMEM] * 7,
        scratch_shapes=[
            pltpu.VMEM((COMP * RHS * PITCH, NZ), F32),
            pltpu.VMEM((NX, NY, NZ), jnp.int32),
            pltpu.SemaphoreType.DMA((2 + COMP,)),
        ],
        compiler_params=params(5),
        name="pack",
    )(edge, far(flat), far(permeability), far(tissue_mask))

    tall, wide = lax.axis_size("gx") * lax.axis_size("gz"), lax.axis_size("gy")

    def gram(index, current, older, before):
        inputs = [current, *(older if index < S else older[-1:]), *before]
        return pl.pallas_call(
            lambda *refs: gram_kernel(index, *refs),
            out_shape=(
                near(COMP, NX, NY, 16, NZ, dtype=BF16),
                near(8, NZ) if index < S else near(wide, 8, NZ),
            ),
            in_specs=[VMEM] * len(inputs),
            out_specs=[VMEM] * 2,
            compiler_params=params(5),
            cost_estimate=pl.CostEstimate(
                flops=2 * 16 * 16 * (index + 1) * 32768, bytes_accessed=(3 + index) << 20, transcendentals=0
            ),
            name=f"gram{index}",
        )(*inputs)

    halo = exchange(sends)
    splits = []
    plane = near(COMP, NX, NY, NZ)
    double = near(2 * COMP, NX, NY, NZ)
    sol, *coef = pl.pallas_call(
        prepare_kernel,
        out_shape=(near(total, NZ), double, double, double, plane, near(6, NX, NY, NZ)),
        in_specs=[SMEM, VMEM] + [in_hbm] * 3,
        out_specs=[VMEM] * 6,
        scratch_shapes=[pltpu.VMEM((NX, NY, NZ), jnp.int32), pltpu.SemaphoreType.DMA((3,))],
        compiler_params=params(5),
        name="prepare",
    )(exchange_table, inner, far(solution.reshape(total, NZ)), far(storage), far(tissue_label))

    def local(index, current):
        return pl.pallas_call(
            lambda *refs: local_kernel(index, *refs),
            out_shape=field,
            in_specs=[VMEM] * 6,
            out_specs=VMEM,
            compiler_params=params(5),
            cost_estimate=pl.CostEstimate(flops=6 << 20, bytes_accessed=3 << 20, transcendentals=0),
            name=f"local{index + 1}",
        )(current, *coef)

    part = local(0, v0)
    split, piece = gram(0, v0, [], [])
    splits.append(split)
    face = near(FACE, 8, NZ)
    results = pl.pallas_call(
        first_kernel,
        out_shape=[field] + [face] * 5 + [near(2, COMP, NY, NZ), near(2, COMP, NX, NZ), plane],
        in_specs=[SMEM] + [VMEM] * 9,
        out_specs=[VMEM] * 9,
        compiler_params=params(5),
        name="step1",
    )(edge, part, v0, inner, *halo)
    current, sends, faces = results[0], results[1:6], results[6:]
    for index in range(1, S):
        halo = exchange(sends)
        part = local(index, current)
        split, piece = gram(index, current, splits, [piece])
        splits.append(split)
        outs = [field] + ([face] * 5 if index < S - 1 else [])
        results = pl.pallas_call(
            step_kernel,
            out_shape=outs,
            in_specs=[SMEM] + [VMEM] * 12,
            out_specs=[VMEM] * len(outs),
                compiler_params=params(5),
            name=f"step{index + 1}",
        )(edge, piece, part, current, *halo, *faces)
        current, sends = results[0], results[1:]
    split, piece = gram(S, current, splits, [piece])
    splits.append(split)
    parts = lax.all_to_all(piece, ("gy",), 0, 0)
    parts = pl.pallas_call(
        relay_kernel,
        out_shape=near(tall, 8, NZ),
        in_specs=[VMEM],
        out_specs=VMEM,
        compiler_params=params(2),
        name="relay",
    )(parts)
    packed = lax.all_to_all(parts, ("gx", "gz"), 0, 0)
    count = COMP * RHS
    new_sol, new_res, basis = pl.pallas_call(
        finish_kernel,
        out_shape=(shaped(count, NX * NY, NZ), shaped(count, NX * NY, NZ), shaped(S * count, NX * NY, NZ)),
        in_specs=[VMEM] * 8,
        out_specs=[in_hbm] * 3,
        scratch_shapes=[
            pltpu.VMEM((count * PITCH, NZ), F32),
            pltpu.VMEM((count * PITCH, NZ), F32),
            pltpu.VMEM((S * count * PITCH, NZ), F32),
            pltpu.VMEM((96, NZ), BF16),
            pltpu.SemaphoreType.DMA((COMP, 3)),
        ],
        compiler_params=params(24),
        name="finish",
    )(packed, *splits, sol, v0)
    return (
        new_sol.reshape(solution.shape),
        new_res.reshape(residual.shape),
        basis.reshape((COMP, S * RHS) + solution.shape[2:]),
    )


def solution(mesh):
    wide = P(None, None, "gx", "gy", "gz")
    return jax.shard_map(
        body,
        mesh=mesh,
        in_specs=(
            wide,
            wide,
            P(None, "gx", "gy", "gz"),
            P(None, "gx", "gy", "gz"),
            P("gx", "gy", "gz"),
            P("gx", "gy", "gz"),
            P(),
        ),
        out_specs=(wide, wide, wide),
        check_vma=False,
    )
```
